128 devices in a mesh: blk: 16 (over z_lo, x, core), narrow: 8 (over z_hi, y).
Axes of the slice: x: 4, y: 4, z: 4 (z_hi: 2, z_lo: 2; z = z_hi * 2 + z_lo), core: 2. Of those that a mesh axis runs over, the one named last changes fastest.
Arguments:
- queries: bfloat16 [512, 8192], P('blk'), may hold values from -181 to 181
- tree_key_cache: bfloat16 [64, 1024, 512], P('blk', 'narrow'), may hold values from -6.1 to 6.1
- tree_value_cache: bfloat16 [64, 1024, 512], P('blk', 'narrow'), may hold values from -8 to 8
- tree_mask: int32 [512, 64], P('blk'), may hold values from 0 to 1, as said below
- lengths: int32 [512], P('blk'), may hold values from 1 to 65536, as said below
- out_weight: bfloat16 [8192, 4096], P('blk', 'narrow'), may hold values from -0.0625 to 0.0625
- residual: bfloat16 [512, 4096], P('blk', 'narrow'), may hold values from -4 to 4
- norm_gain: float32 [4096], P('narrow'), may hold values from 0.1 to 1.9
- expert_ids: int32 [512, 8], P('blk'), may hold values from 0 to 63, all different within a row; in each aligned block of 32 rows (0 to 31, 32 to 63, ...) at most 6 rows name the same one
- gate_weights: float32 [512, 8], P('blk'), may hold values from 0.05 to 0.5
- gate_proj: bfloat16 [64, 4096, 1536], P('blk', 'narrow'), may hold values from -0.09375 to 0.09375
- up_proj: bfloat16 [64, 4096, 1536], P('blk', 'narrow'), may hold values from -0.09375 to 0.09375
- down_proj: bfloat16 [64, 1536, 4096], P('blk', None, 'narrow'), may hold values from -0.15625 to 0.15625
Outputs:
- mixed: bfloat16 [512, 4096], P('blk', 'narrow')
The draws below stay inside these ranges and needn't reach their ends.
Inputs may be any that keep to these rules, and one draw needn't show every extreme that they name: `tree_mask`: block 0 is the root of a tree of 64 blocks in which every other block's parent has a smaller index; row b is 1 exactly on the path from the root to one block, branch b's deepest block. lengths[b] exceeds 1024 times the index of branch b's deepest block by 1 to 1024. `expert_ids`: the 8 entries of a row differ; among the 32 rows of one index of blk no expert is named more than 6 times.
All inputs are finite; a program needn't handle non-finite values.
Results may differ from the reference program's by a relative error of at most 0.025.
Values may be sent and summed in bfloat16 or wider, within the bound.
No kernel may reach another device: no remote copies, remote signals or barrier semaphores. Data moves between devices by JAX's collectives and lax.ppermute only.
A program may use at most 128 MiB of HBM per device.

```python
import math
import jax
import jax.numpy as jnp
import numpy as np
from jax import lax

D = 4096
QUERY_HEADS = 64
KEY_VALUE_HEADS = 4
HEAD_SIZE = 128
FF = 1536
TOP = 8
EXPERTS = 64
BR_DEV = 32
BRANCH_TOTAL = 512
BLOCK_TOKENS = 1024
TREE_BLOCKS = 64
CAP = 6
N_BLK = 16


def tree_draw(key):
    parent_key, leaf_key, offset_key = jax.random.split(key, 3)
    block_ids = jnp.arange(TREE_BLOCKS)
    lowest = block_ids // 4
    parent = jax.random.randint(parent_key, (TREE_BLOCKS,), lowest, jnp.maximum(block_ids, lowest + 1))
    leaf_block = jax.random.randint(leaf_key, (BRANCH_TOTAL,), 0, TREE_BLOCKS)
    leaf_block = leaf_block.at[0].set(TREE_BLOCKS - 1).at[1].set(0)
    offset = jax.random.randint(offset_key, (BRANCH_TOTAL,), 1, BLOCK_TOKENS + 1)
    offset = offset.at[0].set(BLOCK_TOKENS).at[1].set(1)

    def climb(depth_step, loop_carry):
        visited, current = loop_carry
        visited = visited | (current[:, None] == block_ids[None, :])
        return (visited, parent[current])
    visited, current = lax.fori_loop(0, TREE_BLOCKS, climb, (jnp.zeros((BRANCH_TOTAL, TREE_BLOCKS), jnp.bool_), leaf_block))
    return (visited.astype(jnp.int32), (leaf_block * BLOCK_TOKENS + offset).astype(jnp.int32))


def key_field(key):
    return jnp.clip(jax.random.normal(key, (TREE_BLOCKS, BLOCK_TOKENS, KEY_VALUE_HEADS * HEAD_SIZE), jnp.float32), -6.0, 6.0)


def draw_tree_mask(key, part):
    return tree_draw(key)[0]


def draw_lengths(key, part):
    return tree_draw(key)[1]


def draw_tree_key_cache(key, part):
    value_field = key_field(key)
    return value_field.astype(jnp.bfloat16)


def draw_queries(key, part):
    key = jax.random.fold_in(key, 7)
    samples = jnp.clip(jax.random.normal(key, (BRANCH_TOTAL, QUERY_HEADS * HEAD_SIZE), jnp.float32), -6.0, 6.0)
    return samples.astype(jnp.bfloat16)


def draw_tree_value_cache(key, part):
    key = jax.random.fold_in(key, 5)
    jitter_random_key, depth_random_key = jax.random.split(key)
    random_jitter = jax.random.normal(jitter_random_key, (TREE_BLOCKS, BLOCK_TOKENS, KEY_VALUE_HEADS * HEAD_SIZE), jnp.float32)
    block_depth = jax.random.normal(depth_random_key, (TREE_BLOCKS, 1, KEY_VALUE_HEADS * HEAD_SIZE), jnp.float32)
    return jnp.clip(random_jitter + block_depth, -8.0, 8.0).astype(jnp.bfloat16)


def shard_levels(stream_key, dims, pieces, smallest, high):
    def one(dim, parts):
        steps = jax.random.uniform(jax.random.fold_in(jax.random.fold_in(stream_key, 6), dim), (parts,), jnp.float32, smallest / len(pieces), high / len(pieces))
        return jnp.repeat(jnp.exp(steps), dims[dim] // parts).reshape((-1,) + (1,) * (len(dims) - dim - 1))

    factor_of = one(*pieces[0])
    for cut in pieces[1:]:
        factor_of = factor_of * one(*cut)
    return factor_of


def deal_out(stream_key, own, number, rows, number_of, top, bound, slope):
    sequence = jax.random.permutation(stream_key, number_of)
    heavy_load, ordinary = portions_of(number_of, rows * top, bound, slope, True), portions_of(number_of, rows * top, bound, slope, False)
    places = jnp.arange(number_of)

    def named(tallies, turn):
        used = int((tallies > 0).sum())
        fixed = max(1, used // 4)
        shifted = fixed + (places - fixed + turn * (used - fixed)) % max(1, number_of - fixed)
        return jnp.zeros((number_of,), jnp.int32).at[sequence[jnp.where(places < fixed, places, shifted)]].set(jnp.asarray(tallies, jnp.int32))

    tallies = jnp.where(number % 4 == 0, named(heavy_load, number // 4), named(ordinary, number - number // 4 - 1))
    mixed = jax.random.permutation(jax.random.fold_in(own, 3), number_of)
    giver, receiver = mixed[0:number_of // 2 * 2:2], mixed[1:number_of // 2 * 2:2]
    margin = jnp.minimum(tallies[giver] - 1, bound - tallies[receiver]) // 2
    margin = jnp.where((giver == sequence[0]) | (receiver == sequence[0]) | (tallies[receiver] == 0), 0, jnp.maximum(margin, 0))
    shifted = jax.random.randint(jax.random.fold_in(own, 4), (number_of // 2,), 0, 1 << 20) % (margin + 1)
    tallies = tallies.at[giver].add(-shifted).at[receiver].add(shifted)
    members = jnp.searchsorted(jnp.cumsum(tallies), jnp.arange(rows * top), side="right").astype(jnp.int32)
    listing = members.reshape(top, rows).T
    listing = listing[jax.random.permutation(jax.random.fold_in(own, 1), rows)]
    turn = jax.random.randint(jax.random.fold_in(own, 2), (rows, 1), 0, top)
    return jnp.take_along_axis(listing, (jnp.arange(top)[None, :] + turn) % top, axis=1)


def portions_of(amount, total, limit, slope, full):
    weights = [(1 << 20) // math.isqrt(rank ** slope) + 1 for rank in range(1, amount + 1)]
    largest = limit if full else min(limit, max(-(-total // amount), total * weights[0] // sum(weights)))
    least = 1 if total - largest >= amount - 1 else 0
    holding, surplus = [largest] + [least] * (amount - 1), total - largest - least * (amount - 1)
    while surplus > 0:
        movable = [i for i in range(1, amount) if holding[i] < largest] or [i for i in range(1, amount) if holding[i] < limit]
        whole, remaining = sum([weights[i] for i in movable]), surplus
        for i in movable:
            more = min(limit - holding[i], max(1, remaining * weights[i] // whole), surplus)
            holding[i] = holding[i] + more
            surplus = surplus - more
    return np.array(holding)


def bell_draw(own_key, dims, deviation, most, cuts=(), kind=jnp.bfloat16):
    gain = shard_levels(own_key, dims, cuts, -0.22, 0.18) if cuts else 1.0
    result = jax.random.normal(own_key, dims, jnp.float32) * deviation * gain
    return jnp.minimum(jnp.maximum(result, -most), most).astype(kind)


def setup_inputs(seed: int = 0) -> dict:
    streams_of = jax.random.split(jax.random.key(seed), 14)
    queries = draw_queries(jax.random.fold_in(streams_of[13], 71), 0)
    tree_key_cache = draw_tree_key_cache(jax.random.fold_in(streams_of[13], 71), 0)
    tree_value_cache = draw_tree_value_cache(jax.random.fold_in(streams_of[13], 71), 0)
    tree_mask = draw_tree_mask(jax.random.fold_in(streams_of[13], 71), 0)
    lengths = draw_lengths(jax.random.fold_in(streams_of[13], 71), 0)
    out_weight = bell_draw(streams_of[5], (QUERY_HEADS * HEAD_SIZE, D), (QUERY_HEADS * HEAD_SIZE) ** -0.5, 0.0625, ((0, 16), (1, 8)))
    residual = bell_draw(streams_of[6], (BRANCH_TOTAL, D), 0.5, 4.0, ((0, 16), (1, 8)))
    norm_gain = jnp.clip(1.0 + 0.18 * jax.random.normal(streams_of[7], (D,), jnp.float32), 0.1, 1.9)
    expert_ids_keys = jax.random.split(jax.random.fold_in(streams_of[8], 1), BRANCH_TOTAL // BR_DEV)
    expert_ids_turns = jax.random.permutation(jax.random.fold_in(streams_of[8], 3), BRANCH_TOTAL // BR_DEV)
    expert_ids = jax.vmap(lambda own, number: deal_out(jax.random.fold_in(streams_of[8], 2), own, number, BR_DEV, EXPERTS, TOP, CAP, 2))(expert_ids_keys, expert_ids_turns).reshape((BRANCH_TOTAL, TOP))
    gate_weights = jnp.clip(jnp.exp(math.log(0.5) - 2.3025851 * jax.random.uniform(streams_of[9], (BRANCH_TOTAL, TOP), jnp.float32) ** shard_levels(streams_of[9], (BRANCH_TOTAL, TOP), ((0, 16),), -0.2, 0.2)), 0.05, 0.5)
    gate_proj = bell_draw(streams_of[10], (EXPERTS, D, FF), D ** -0.5, 0.09375, ((0, 16), (1, 8)))
    up_proj = bell_draw(streams_of[11], (EXPERTS, D, FF), D ** -0.5, 0.09375, ((0, 16), (1, 8)))
    down_proj = bell_draw(streams_of[12], (EXPERTS, FF, D), FF ** -0.5, 0.15625, ((0, 16), (2, 8)))
    return {"queries": queries, "tree_key_cache": tree_key_cache, "tree_value_cache": tree_value_cache, "tree_mask": tree_mask, "lengths": lengths, "out_weight": out_weight, "residual": residual, "norm_gain": norm_gain, "expert_ids": expert_ids, "gate_weights": gate_weights, "gate_proj": gate_proj, "up_proj": up_proj, "down_proj": down_proj}


NEGATIVE_FILLER = -1e+30
EPSILON = 1e-06

def reference(queries, tree_key_cache, tree_value_cache, tree_mask, lengths, out_weight, residual, norm_gain, expert_ids, gate_weights, gate_proj, up_proj, down_proj):
    total_tokens = TREE_BLOCKS * BLOCK_TOKENS
    heads_per_group = QUERY_HEADS // KEY_VALUE_HEADS
    flattened_keys = tree_key_cache.reshape(total_tokens, KEY_VALUE_HEADS, HEAD_SIZE).astype(jnp.float32)
    flattened_values = tree_value_cache.reshape(total_tokens, KEY_VALUE_HEADS, HEAD_SIZE).astype(jnp.float32)
    positions = jnp.arange(total_tokens)
    tok_block = positions // BLOCK_TOKENS

    def attend(group):
        query_matrix, mask_rows, length_rows = group
        query_head_rows = query_matrix.astype(jnp.float32).reshape(-1, KEY_VALUE_HEADS, heads_per_group, HEAD_SIZE)
        scores = jnp.einsum('rkgd,tkd->rkgt', query_head_rows, flattened_keys) * HEAD_SIZE ** (-0.5)
        readable = (mask_rows[:, tok_block] == 1) & (positions[None, :] < length_rows[:, None])
        live_mask = readable[:, None, None, :]
        scores = jnp.where(live_mask, scores, NEGATIVE_FILLER)
        row_max = lax.optimization_barrier(jnp.max(scores, axis=-1))
        weights = jnp.where(live_mask, jnp.exp(scores - row_max[..., None]), 0.0)
        denominator = lax.optimization_barrier(jnp.sum(weights, axis=-1))
        rounded = lax.optimization_barrier(weights.astype(jnp.bfloat16)).astype(jnp.float32)
        summed = jnp.einsum('rkgt,tkd->rkgd', rounded, flattened_values)
        return (summed / denominator[..., None]).reshape(-1, QUERY_HEADS * HEAD_SIZE).astype(jnp.bfloat16)
    group_rows = math.gcd(BR_DEV, 32)
    attended = lax.map(attend, (queries.reshape(-1, group_rows, QUERY_HEADS * HEAD_SIZE), tree_mask.reshape(-1, group_rows, TREE_BLOCKS), lengths.reshape(-1, group_rows)))
    attended = attended.reshape(BRANCH_TOTAL, QUERY_HEADS * HEAD_SIZE)
    projected = jnp.dot(attended, out_weight, preferred_element_type=jnp.float32)
    hidden_b = (residual.astype(jnp.float32) + projected).astype(jnp.bfloat16)
    ids_group = expert_ids.reshape(N_BLK, BR_DEV * TOP)
    expert_hot = (ids_group[..., None] == jnp.arange(EXPERTS)[None, None, :]).astype(jnp.int32)
    earlier = jnp.cumsum(expert_hot, axis=1) - expert_hot
    slot_of = lax.optimization_barrier(jnp.sum(earlier * expert_hot, axis=2))
    source = jnp.arange(N_BLK)[:, None]
    target = ((ids_group * N_BLK + source) * CAP + slot_of).reshape(-1).astype(jnp.int32)
    token_of = (jnp.arange(BRANCH_TOTAL * TOP) // TOP).astype(jnp.int32)
    slot_rows = EXPERTS * N_BLK * CAP
    buffer_idx = jnp.full((slot_rows,), BRANCH_TOTAL, jnp.int32).at[target].set(token_of)
    padded = jnp.concatenate([hidden_b, jnp.zeros((1, D), jnp.bfloat16)], axis=0)
    inputs_e = padded[buffer_idx].reshape(EXPERTS, N_BLK * CAP, D)

    def expert(group):
        rows_in, gate_mat, up_mat, down_mat = group
        wide_rows = rows_in.astype(jnp.float32)
        inv_rms = lax.rsqrt(lax.optimization_barrier(jnp.sum(wide_rows * wide_rows, axis=-1, keepdims=True)) / D + EPSILON)
        scaled = (wide_rows * norm_gain).astype(jnp.bfloat16)
        gate_val = jnp.dot(scaled, gate_mat, preferred_element_type=jnp.float32) * inv_rms
        up_val = jnp.dot(scaled, up_mat, preferred_element_type=jnp.float32) * inv_rms
        activated = (jax.nn.silu(gate_val) * up_val).astype(jnp.bfloat16)
        return jnp.dot(activated, down_mat, preferred_element_type=jnp.float32).astype(jnp.bfloat16)
    outputs = lax.map(expert, (inputs_e, gate_proj, up_proj, down_proj)).reshape(slot_rows, D)
    picked = outputs[target].reshape(BRANCH_TOTAL, TOP, D)
    mixed_in = lax.optimization_barrier(jnp.sum(gate_weights[..., None] * picked.astype(jnp.float32), axis=1))
    return (hidden_b.astype(jnp.float32) + mixed_in).astype(jnp.bfloat16)
```

```python
import functools

import jax
import jax.numpy as jnp
from jax import lax
from jax.experimental import pallas as pl
from jax.experimental.pallas import tpu as pltpu
from jax.sharding import PartitionSpec as P

D = 4096
QUERY_HEADS = 64
KEY_VALUE_HEADS = 4
HEAD_SIZE = 128
FF = 1536
TOP = 8
CAP = 6
BLOCK_TOKENS = 1024
TREE_BLOCKS = 64
NEGATIVE_FILLER = -1e30
EPSILON = 1e-06
SCORE_SCALE = HEAD_SIZE ** (-0.5)
LOG2E = 1.4426950408889634
LANES = 128
VMEM_LIMIT = 56 * 1024 * 1024


def params(*semantics):
    return pltpu.CompilerParams(dimension_semantics=semantics, vmem_limit_bytes=VMEM_LIMIT)


def split_bf16(value):
    high = value.astype(jnp.bfloat16)
    rest = value - high.astype(jnp.float32)
    mid = rest.astype(jnp.bfloat16)
    low = (rest - mid.astype(jnp.float32)).astype(jnp.bfloat16)
    return high, mid, low


def gather_by_exchange(value, axis):
    length = lax.axis_size(axis)
    spread = jnp.broadcast_to(value[None], (length,) + value.shape)
    return lax.all_to_all(spread, axis, 0, 0)


def attention_kernel(heads, blocks, q_ref, lim_ref, kv_ref, out_ref, kt_ref, v_ref, s_ref):
    rows = q_ref.shape[0]
    parts = kv_ref.shape[0]

    @pl.when(pl.program_id(0) == 0)
    def _():
        lane = lax.broadcasted_iota(jnp.int32, (BLOCK_TOKENS, HEAD_SIZE), 1)
        ones = jnp.where(lane == 0, 1.0, 0.0).astype(jnp.bfloat16)
        for i in range(blocks):
            span = pl.ds(i * BLOCK_TOKENS, BLOCK_TOKENS)
            keys = kv_ref[:, 0, i].reshape(BLOCK_TOKENS, HEAD_SIZE)
            kt_ref[:, span] = keys.T
            v_ref[span, :HEAD_SIZE] = kv_ref[:, 1, i].reshape(BLOCK_TOKENS, HEAD_SIZE)
            v_ref[span, HEAD_SIZE:] = ones

    token = lax.broadcasted_iota(jnp.int32, (rows, BLOCK_TOKENS), 1)
    lane_row = lax.broadcasted_iota(jnp.int32, (rows, LANES), 1)

    def one_head(h, info):
        cols = pl.ds(pl.multiple_of(h * HEAD_SIZE, HEAD_SIZE), HEAD_SIZE)
        q = q_ref[:, cols]
        top = jnp.full((rows, 1), -1e29, jnp.float32)
        for i in range(blocks):
            span = pl.ds(i * BLOCK_TOKENS, BLOCK_TOKENS)
            s = jnp.dot(q, kt_ref[:, span], preferred_element_type=jnp.float32)
            s = jnp.where(token < lim_ref[:, i : i + 1], s, NEGATIVE_FILLER)
            s_ref[:, span] = s
            top = jnp.maximum(top, jnp.max(s, axis=1, keepdims=True))
        acc = jnp.zeros((rows, 2 * HEAD_SIZE), jnp.float32)
        for i in range(blocks):
            span = pl.ds(i * BLOCK_TOKENS, BLOCK_TOKENS)
            p = jnp.exp2((s_ref[:, span] - top) * (SCORE_SCALE * LOG2E)).astype(jnp.bfloat16)
            acc = acc + jnp.dot(p, v_ref[span, :], preferred_element_type=jnp.float32)
        total = acc[:, HEAD_SIZE : HEAD_SIZE + 1]
        some = total > 0
        safe = jnp.where(some, total, 1.0)
        out_ref[:, cols] = (acc[:, :HEAD_SIZE] / safe).astype(jnp.bfloat16)
        lse = jnp.where(some, top * SCORE_SCALE + jnp.log(safe), NEGATIVE_FILLER)
        return jnp.where(lane_row == h, lse, info)

    info = lax.fori_loop(0, heads, one_head, jnp.zeros((rows, LANES), jnp.float32))
    high, mid, low = split_bf16(info[:, :heads])
    base = heads * HEAD_SIZE
    out_ref[:, base:] = jnp.zeros((rows, LANES), jnp.bfloat16)
    out_ref[:, base : base + heads] = high
    out_ref[:, base + heads : base + 2 * heads] = mid
    out_ref[:, base + 2 * heads : base + 3 * heads] = low


def attention(queries, limits, kv):
    total_rows, width = queries.shape
    heads = width // HEAD_SIZE
    blocks = kv.shape[2]
    rows = 256
    tokens = blocks * BLOCK_TOKENS
    return pl.pallas_call(
        functools.partial(attention_kernel, heads, blocks),
        grid=(total_rows // rows,),
        in_specs=[
            pl.BlockSpec((rows, width), lambda r: (r, 0)),
            pl.BlockSpec((rows, blocks), lambda r: (r, 0)),
            pl.BlockSpec(kv.shape, lambda r: (0, 0, 0, 0, 0)),
        ],
        out_specs=pl.BlockSpec((rows, width + LANES), lambda r: (r, 0)),
        out_shape=jax.ShapeDtypeStruct((total_rows, width + LANES), jnp.bfloat16),
        scratch_shapes=[
            pltpu.VMEM((HEAD_SIZE, tokens), jnp.bfloat16),
            pltpu.VMEM((tokens, 2 * HEAD_SIZE), jnp.bfloat16),
            pltpu.VMEM((rows, tokens), jnp.float32),
        ],
        compiler_params=params("arbitrary"),
        cost_estimate=pl.CostEstimate(
            flops=6 * total_rows * heads * tokens * HEAD_SIZE,
            bytes_accessed=6 << 20,
            transcendentals=total_rows * heads * tokens,
        ),
        name="attention",
    )(queries, limits, kv)


def combine_kernel(heads, x_ref, out_ref):
    base = heads * HEAD_SIZE
    info = x_ref[:, :, base:].astype(jnp.float32)
    half = out_ref.shape[2] // HEAD_SIZE
    for h in range(heads):
        lse = info[:, :, h : h + 1] + info[:, :, heads + h : heads + h + 1]
        lse = lse + info[:, :, 2 * heads + h : 2 * heads + h + 1]
        scale = jnp.exp(lse - jnp.max(lse, axis=0, keepdims=True))
        cols = slice(h * HEAD_SIZE, (h + 1) * HEAD_SIZE)
        acc = jnp.sum(x_ref[:, :, cols].astype(jnp.float32) * scale, axis=0)
        acc = acc / jnp.sum(scale, axis=0)
        at = (h % half) * HEAD_SIZE
        out_ref[h // half, :, at : at + HEAD_SIZE] = acc.astype(jnp.bfloat16)


def combine(parts, heads):
    count, rows, _ = parts.shape
    return pl.pallas_call(
        functools.partial(combine_kernel, heads),
        out_shape=jax.ShapeDtypeStruct((2, rows, heads * HEAD_SIZE // 2), jnp.bfloat16),
        compiler_params=params(),
        name="combine",
    )(parts)


def gate_up_kernel(tiles, x_ref, perm_ref, gain_ref, gate_ref, up_ref, out_ref, scaled_ref):
    f = pl.program_id(1)
    width = gate_ref.shape[1]

    @pl.when(f == 0)
    def _():
        rows = jnp.dot(perm_ref[...], x_ref[...], preferred_element_type=jnp.float32)
        scaled_ref[...] = (rows * gain_ref[...]).astype(jnp.bfloat16)
        squares = jnp.sum(rows * rows, axis=1, keepdims=True)
        high, mid, _ = split_bf16(squares)
        lane = lax.broadcasted_iota(jnp.int32, (rows.shape[0], LANES), 1)
        pad = jnp.where(lane == 0, high.astype(jnp.float32), 0.0)
        pad = jnp.where(lane == 1, mid.astype(jnp.float32), pad)
        out_ref[:, 2 * tiles * width :] = pad.astype(jnp.bfloat16)

    scaled = scaled_ref[...]
    at = pl.multiple_of(f * width, LANES)
    out_ref[:, pl.ds(at, width)] = jnp.dot(
        scaled, gate_ref[...], preferred_element_type=jnp.float32
    ).astype(jnp.bfloat16)
    out_ref[:, pl.ds(tiles * width + at, width)] = jnp.dot(
        scaled, up_ref[...], preferred_element_type=jnp.float32
    ).astype(jnp.bfloat16)


def gate_up(x, perm, gain, gate_proj, up_proj):
    experts, depth, ff = gate_proj.shape
    slots = x.shape[0]
    rows = slots // experts
    tiles = 3
    width = ff // tiles
    weight_spec = pl.BlockSpec((None, depth, width), lambda e, f: (e, 0, f))
    return pl.pallas_call(
        functools.partial(gate_up_kernel, tiles),
        grid=(experts, tiles),
        in_specs=[
            pl.BlockSpec((slots, depth), lambda e, f: (0, 0)),
            pl.BlockSpec((rows, slots), lambda e, f: (e, 0)),
            pl.BlockSpec((1, depth), lambda e, f: (0, 0)),
            weight_spec,
            weight_spec,
        ],
        out_specs=pl.BlockSpec((rows, 2 * ff + LANES), lambda e, f: (e, 0)),
        out_shape=jax.ShapeDtypeStruct((slots, 2 * ff + LANES), jnp.bfloat16),
        scratch_shapes=[pltpu.VMEM((rows, depth), jnp.bfloat16)],
        compiler_params=params("arbitrary", "arbitrary"),
        cost_estimate=pl.CostEstimate(
            flops=4 * slots * depth * ff,
            bytes_accessed=4 * experts * depth * ff + 8 * slots * ff,
            transcendentals=0,
        ),
        name="gate_up",
    )(x, perm, gain, gate_proj, up_proj)


def activate_kernel(x_ref, out_ref):
    ff = out_ref.shape[1]
    rows = out_ref.shape[0]
    parts = x_ref.shape[0]
    squares = jnp.zeros((rows, 1), jnp.float32)
    for part in range(parts):
        pad = x_ref[part, :, 2 * ff :].astype(jnp.float32)
        squares = squares + pad[:, 0:1] + pad[:, 1:2]
    inv_rms = lax.rsqrt(squares / D + EPSILON)
    step = 256
    for at in range(0, ff, step):
        gate = jnp.zeros((rows, step), jnp.float32)
        up = jnp.zeros((rows, step), jnp.float32)
        for part in range(parts):
            gate = gate + x_ref[part, :, at : at + step].astype(jnp.float32)
            up = up + x_ref[part, :, ff + at : ff + at + step].astype(jnp.float32)
        gate = gate * inv_rms
        up = up * inv_rms
        out_ref[:, at : at + step] = (gate / (1.0 + jnp.exp(-gate)) * up).astype(jnp.bfloat16)


def activate(parts):
    _, rows, width = parts.shape
    return pl.pallas_call(
        activate_kernel,
        out_shape=jax.ShapeDtypeStruct((rows, (width - LANES) // 2), jnp.bfloat16),
        compiler_params=params(),
        name="activate",
    )(parts)


def down_kernel(act_ref, perm_ref, down_ref, out_ref, acc_ref):
    e = pl.program_id(0)
    piece = jnp.dot(act_ref[...], down_ref[...], preferred_element_type=jnp.float32)
    piece = jnp.dot(
        perm_ref[...].T, piece.astype(jnp.bfloat16), preferred_element_type=jnp.float32
    )

    @pl.when(e == 0)
    def _():
        acc_ref[...] = piece

    @pl.when(e > 0)
    def _():
        acc_ref[...] += piece

    @pl.when(e == pl.num_programs(0) - 1)
    def _():
        out_ref[...] = acc_ref[...].astype(jnp.bfloat16)


def down(act, perm, down_proj):
    experts, ff, width = down_proj.shape
    slots = act.shape[0]
    rows = slots // experts
    return pl.pallas_call(
        down_kernel,
        grid=(experts,),
        in_specs=[
            pl.BlockSpec((rows, ff), lambda e: (e, 0)),
            pl.BlockSpec((rows, slots), lambda e: (e, 0)),
            pl.BlockSpec((None, ff, width), lambda e: (e, 0, 0)),
        ],
        out_specs=pl.BlockSpec((slots, width), lambda e: (0, 0)),
        out_shape=jax.ShapeDtypeStruct((slots, width), jnp.bfloat16),
        scratch_shapes=[pltpu.VMEM((slots, width), jnp.float32)],
        compiler_params=params("arbitrary"),
        cost_estimate=pl.CostEstimate(
            flops=2 * slots * ff * width,
            bytes_accessed=2 * experts * ff * width,
            transcendentals=0,
        ),
        name="down",
    )(act, perm, down_proj)


def per_device(
    queries,
    tree_key_cache,
    tree_value_cache,
    tree_mask,
    lengths,
    out_weight,
    residual,
    norm_gain,
    expert_ids,
    gate_weights,
    gate_proj,
    up_proj,
    down_proj,
):
    rows = queries.shape[0]
    blocks, part_tokens = tree_key_cache.shape[:2]
    n_blk = lax.axis_size("blk")
    n_narrow = lax.axis_size("narrow")
    my_blk = lax.axis_index("blk")
    my_part = lax.axis_index("narrow")
    heads = QUERY_HEADS // n_narrow
    sharing = n_narrow // KEY_VALUE_HEADS

    first = jnp.arange(TREE_BLOCKS) * BLOCK_TOKENS
    bound = jnp.clip(lengths[:, None] - first[None, :], 0, BLOCK_TOKENS)
    bound = jnp.where(tree_mask == 1, bound, 0)
    own_q = lax.dynamic_slice_in_dim(queries, my_part * heads * HEAD_SIZE, heads * HEAD_SIZE, 1)
    q_out = jnp.concatenate(
        [own_q, (bound // 32).astype(jnp.bfloat16), (bound % 32).astype(jnp.bfloat16)], axis=1
    )
    q_all = lax.all_gather(q_out, "blk", tiled=True)

    kv = jnp.stack([tree_key_cache, tree_value_cache])
    kv = kv.reshape(2, blocks, part_tokens, KEY_VALUE_HEADS, HEAD_SIZE)
    kv = jnp.repeat(kv.transpose(3, 0, 1, 2, 4), sharing, axis=0)
    kv = lax.all_to_all(kv, "narrow", 0, 0)

    width = heads * HEAD_SIZE
    bounds = (q_all[:, width : width + TREE_BLOCKS].astype(jnp.int32) * 32) + q_all[
        :, width + TREE_BLOCKS :
    ].astype(jnp.int32)
    limits = lax.dynamic_slice_in_dim(bounds, my_blk * blocks, blocks, 1)
    partial = attention(q_all[:, :width], limits, kv)
    partial = lax.all_to_all(partial.reshape(n_blk, rows, width + LANES), "blk", 0, 0)
    attended = combine(partial, heads)
    attended = gather_by_exchange(attended, "narrow")
    attended = attended.reshape(n_blk, rows, QUERY_HEADS * HEAD_SIZE // n_blk)
    attended = lax.all_to_all(attended, "blk", 0, 0)
    projected = jnp.dot(
        attended.reshape(n_blk * rows, -1), out_weight, preferred_element_type=jnp.float32
    ).astype(jnp.bfloat16)
    projected = lax.all_to_all(projected.reshape(n_blk, rows, -1), "blk", 0, 0)
    projected = jnp.sum(projected.astype(jnp.float32), axis=0)
    hidden_b = (residual.astype(jnp.float32) + projected).astype(jnp.bfloat16)

    exp_dev = gate_proj.shape[0]
    n_experts = exp_dev * n_blk
    flat_ids = expert_ids.reshape(-1)
    expert_hot = (flat_ids[:, None] == jnp.arange(n_experts)[None, :]).astype(jnp.int32)
    earlier = jnp.cumsum(expert_hot, axis=0) - expert_hot
    slot_of = jnp.sum(earlier * expert_hot, axis=1)
    target = (flat_ids * CAP + slot_of).reshape(rows, TOP)
    slots = n_experts * CAP
    at_slot = target[:, :, None] == jnp.arange(slots)[None, None, :]
    select = jnp.any(at_slot, axis=1).astype(jnp.bfloat16)
    mixing = jnp.sum(jnp.where(at_slot, gate_weights[:, :, None], 0.0), axis=1)
    outgoing = lax.dot_general(
        select, hidden_b, (((0,), (0,)), ((), ())), preferred_element_type=jnp.float32
    ).astype(jnp.bfloat16)
    incoming = lax.all_to_all(outgoing.reshape(n_blk, exp_dev * CAP, -1), "blk", 0, 0)

    place = jnp.arange(slots)
    expert, rest = place // (n_blk * CAP), place % (n_blk * CAP)
    order = (rest // CAP) * (exp_dev * CAP) + expert * CAP + rest % CAP
    perm = (order[:, None] == place[None, :]).astype(jnp.bfloat16)

    parts = gate_up(
        incoming.reshape(slots, -1), perm, norm_gain.reshape(1, -1), gate_proj, up_proj
    )
    parts = lax.all_to_all(parts.reshape(n_narrow, slots // n_narrow, -1), "narrow", 0, 0)
    activated = gather_by_exchange(activate(parts), "narrow").reshape(slots, -1)
    expert_out = down(activated, perm, down_proj)
    returned = lax.all_to_all(expert_out.reshape(n_blk, exp_dev * CAP, -1), "blk", 0, 0)
    returned = returned.reshape(slots, -1)
    mix_high = lax.reduce_precision(mixing, 8, 7)
    mix_low = mixing - mix_high
    mixed_in = jnp.dot(
        mix_high.astype(jnp.bfloat16), returned, preferred_element_type=jnp.float32
    ) + jnp.dot(mix_low.astype(jnp.bfloat16), returned, preferred_element_type=jnp.float32)
    return (hidden_b.astype(jnp.float32) + mixed_in).astype(jnp.bfloat16)


def solution(mesh):
    in_specs = (
        P("blk", None),
        P("blk", "narrow", None),
        P("blk", "narrow", None),
        P("blk", None),
        P("blk"),
        P("blk", "narrow"),
        P("blk", "narrow"),
        P("narrow"),
        P("blk", None),
        P("blk", None),
        P("blk", "narrow", None),
        P("blk", "narrow", None),
        P("blk", None, "narrow"),
    )
    out_specs = P("blk", "narrow")
    return jax.shard_map(
        per_device, mesh=mesh, in_specs=in_specs, out_specs=out_specs, check_vma=False
    )
```

```python
import functools

import jax
import jax.numpy as jnp
from jax import lax
from jax.experimental import pallas as pl
from jax.experimental.pallas import tpu as pltpu
from jax.sharding import Mesh
from jax.sharding import PartitionSpec as P

D = 4096
QUERY_HEADS = 64
KEY_VALUE_HEADS = 4
HEAD_SIZE = 128
FF = 1536
TOP = 8
CAP = 6
BLOCK_TOKENS = 1024
TREE_BLOCKS = 64
NEGATIVE_FILLER = -1e30
EPSILON = 1e-06
SCORE_SCALE = HEAD_SIZE ** (-0.5)
LOG2E = 1.4426950408889634
LANES = 128
BLK = ("zl", "x", "core")
NARROW = ("zh", "yh", "yl")
VMEM_LIMIT = 32 * 1024 * 1024
SMALL_LIMIT = 12 * 1024 * 1024


def params(limit):
    return pltpu.CompilerParams(vmem_limit_bytes=limit)


def split_bf16(value):
    high = value.astype(jnp.bfloat16)
    rest = value - high.astype(jnp.float32)
    mid = rest.astype(jnp.bfloat16)
    low = (rest - mid.astype(jnp.float32)).astype(jnp.bfloat16)
    return high, mid, low


def gather_by_exchange(value, axis):
    length = lax.axis_size(axis)
    spread = jnp.broadcast_to(value[None], (length,) + value.shape)
    return lax.all_to_all(spread, axis, 0, 0)


def attention_kernel(start, heads, *refs):
    info_ref = refs[0]
    q_refs = refs[1:9]
    kv_refs = refs[9:17]
    out_ref, q_ref, k_ref, vt_ref, lim_ref, s_ref = refs[17:]
    rows = q_ref.shape[0]
    base = q_refs[0].shape[1] - LANES
    chip, core, my_yh = info_ref[0], info_ref[1], info_ref[2]
    sources = len(kv_refs) // 2
    blocks = kv_refs[0].shape[1]
    span = sources * LANES
    step = rows // len(q_refs)

    for i, ref in enumerate(q_refs):
        q_ref[i * step : (i + 1) * step, :] = ref[...]
    extra = q_ref[:, base:].astype(jnp.float32).T
    lim_ref[...] = extra
    length = extra[TREE_BLOCKS : TREE_BLOCKS + 1] * 256.0 + extra[TREE_BLOCKS + 1 : TREE_BLOCKS + 2]
    chip_blocks = 2 * blocks
    first = pl.multiple_of(chip * chip_blocks, chip_blocks)
    mask = lim_ref[pl.ds(first, chip_blocks), :]
    block_id = lax.broadcasted_iota(jnp.int32, (chip_blocks, rows), 0) + first
    bound = length - (block_id * BLOCK_TOKENS).astype(jnp.float32)
    bound = jnp.where(mask > 0.5, bound, 0.0)
    lim_ref[0:chip_blocks, :] = bound
    sub = lax.broadcasted_iota(jnp.int32, (16, blocks * 2 * span), 0)
    vt_ref[HEAD_SIZE:, :] = jnp.where(sub == 0, 1.0, 0.0).astype(jnp.bfloat16)
    for side in range(2):
        for i in range(blocks):
            for s in range(sources):
                at = (side * blocks + i) * span + s * LANES
                ref = kv_refs[side * sources + s]
                k_ref[at : at + LANES, :] = ref[0, i]
                vt_ref[:HEAD_SIZE, at : at + LANES] = ref[1, i].T

    token = lax.broadcasted_iota(jnp.int32, (LANES, 1), 0) + my_yh * (2 * LANES)
    token = [(token + info_ref[4 + s] * LANES).astype(jnp.float32) for s in range(sources)]
    token = jnp.concatenate(token, axis=0)
    sub_row = lax.broadcasted_iota(jnp.int32, (8, rows), 0)

    def one_head(h, info):
        cols = pl.ds(pl.multiple_of(h * HEAD_SIZE, HEAD_SIZE), HEAD_SIZE)
        q_cols = pl.ds(pl.multiple_of((start + h) * HEAD_SIZE, HEAD_SIZE), HEAD_SIZE)
        qt = q_ref[:, q_cols].T
        top = jnp.full((1, rows), -1e29, jnp.float32)
        for i in range(2 * blocks):
            at = slice(i * span, (i + 1) * span)
            side = core if i < blocks else 1 - core
            lim = lim_ref[pl.ds(side * blocks + i % blocks, 1), :]
            s = jnp.dot(k_ref[at, :], qt, preferred_element_type=jnp.float32)
            s = jnp.where(token < lim, s, NEGATIVE_FILLER)
            s_ref[at, :] = s
            top = jnp.maximum(top, jnp.max(s, axis=0, keepdims=True))
        acc = jnp.zeros((HEAD_SIZE + 16, rows), jnp.float32)
        for i in range(2 * blocks):
            at = slice(i * span, (i + 1) * span)
            p = jnp.exp2((s_ref[at, :] - top) * (SCORE_SCALE * LOG2E)).astype(jnp.bfloat16)
            acc = acc + jnp.dot(vt_ref[:, at], p, preferred_element_type=jnp.float32)
        total = acc[HEAD_SIZE : HEAD_SIZE + 1]
        some = total > 0
        safe = jnp.where(some, total, 1.0)
        result = (acc[:HEAD_SIZE] / safe).astype(jnp.bfloat16).T
        group = rows // 16
        for i in range(16):
            row = pl.multiple_of(info_ref[8 + i] * group, group)
            out_ref[pl.ds(row, group), cols] = result[i * group : (i + 1) * group]
        lse = jnp.where(some, top * SCORE_SCALE + jnp.log(safe), NEGATIVE_FILLER)
        return jnp.where(sub_row == h, lse, info)

    info = lax.fori_loop(0, heads, one_head, jnp.zeros((8, rows), jnp.float32))
    high, mid, low = split_bf16(info)
    pieces = [piece.astype(jnp.float32) for piece in (high, mid, low)]
    pieces.append(jnp.zeros((LANES - 24, rows), jnp.float32))
    result = jnp.concatenate(pieces, axis=0).T.astype(jnp.bfloat16)
    group = rows // 16
    for i in range(16):
        row = pl.multiple_of(info_ref[8 + i] * group, group)
        out_ref[pl.ds(row, group), heads * HEAD_SIZE :] = result[i * group : (i + 1) * group]


def attention(info, queries, kv, start, heads):
    step, width = queries[0].shape
    rows = step * len(queries)
    out_width = heads * HEAD_SIZE + LANES
    blocks = kv[0].shape[1]
    tokens = len(kv) * blocks * LANES
    vmem = pl.BlockSpec(memory_space=pltpu.VMEM)
    return pl.pallas_call(
        functools.partial(attention_kernel, start, heads),
        in_specs=[pl.BlockSpec(memory_space=pltpu.SMEM)] + [vmem] * (len(queries) + len(kv)),
        out_specs=vmem,
        out_shape=jax.ShapeDtypeStruct((rows, out_width), jnp.bfloat16),
        scratch_shapes=[
            pltpu.VMEM((rows, width), jnp.bfloat16),
            pltpu.VMEM((tokens, HEAD_SIZE), jnp.bfloat16),
            pltpu.VMEM((HEAD_SIZE + 16, tokens), jnp.bfloat16),
            pltpu.VMEM((LANES, rows), jnp.float32),
            pltpu.VMEM((tokens, rows), jnp.float32),
        ],
        compiler_params=params(limit=VMEM_LIMIT),
        cost_estimate=pl.CostEstimate(
            flops=6 * rows * heads * tokens * HEAD_SIZE,
            bytes_accessed=6 << 20,
            transcendentals=rows * heads * tokens,
        ),
        name="attention",
    )(info, *queries, *kv)


def combine_kernel(heads, x_ref, out_ref):
    base = heads * HEAD_SIZE
    info = x_ref[:, :, base:].astype(jnp.float32)
    for h in range(heads):
        lse = info[:, :, h : h + 1] + info[:, :, 8 + h : 9 + h]
        lse = lse + info[:, :, 16 + h : 17 + h]
        scale = jnp.exp(lse - jnp.max(lse, axis=0, keepdims=True))
        cols = slice(h * HEAD_SIZE, (h + 1) * HEAD_SIZE)
        acc = jnp.sum(x_ref[:, :, cols].astype(jnp.float32) * scale, axis=0)
        out_ref[:, cols] = (acc / jnp.sum(scale, axis=0)).astype(jnp.bfloat16)


def combine(parts, heads):
    _, rows, _ = parts.shape
    return pl.pallas_call(
        functools.partial(combine_kernel, heads),
        out_shape=jax.ShapeDtypeStruct((rows, heads * HEAD_SIZE), jnp.bfloat16),
        compiler_params=params(limit=SMALL_LIMIT),
        cost_estimate=pl.CostEstimate(
            flops=4 * parts.size, bytes_accessed=2 * parts.size, transcendentals=0
        ),
        name="combine",
    )(parts)


def gate_up_kernel(x_ref, perm_ref, gain_ref, gate_ref, up_ref, out_ref):
    experts, _, width = gate_ref.shape
    count = x_ref.shape[0] // experts
    for e in range(experts):
        at = slice(e * count, (e + 1) * count)
        rows = jnp.dot(perm_ref[at, :], x_ref[...], preferred_element_type=jnp.float32)
        scaled = (rows * gain_ref[...]).astype(jnp.bfloat16)
        squares = jnp.sum(rows * rows, axis=1, keepdims=True)
        high, mid, _ = split_bf16(squares)
        lane = lax.broadcasted_iota(jnp.int32, (count, LANES), 1)
        pad = jnp.where(lane == 0, high.astype(jnp.float32), 0.0)
        pad = jnp.where(lane == 1, mid.astype(jnp.float32), pad)
        out_ref[at, 2 * width :] = pad.astype(jnp.bfloat16)
        out_ref[at, :width] = jnp.dot(
            scaled, gate_ref[e], preferred_element_type=jnp.float32
        ).astype(jnp.bfloat16)
        out_ref[at, width : 2 * width] = jnp.dot(
            scaled, up_ref[e], preferred_element_type=jnp.float32
        ).astype(jnp.bfloat16)


def gate_up(x, perm, gain, gate_proj, up_proj):
    experts, depth, ff = gate_proj.shape
    slots = x.shape[0]
    vmem = pl.BlockSpec(memory_space=pltpu.VMEM)
    return pl.pallas_call(
        gate_up_kernel,
        in_specs=[vmem] * 5,
        out_specs=vmem,
        out_shape=jax.ShapeDtypeStruct((slots, 2 * ff + LANES), jnp.bfloat16),
        compiler_params=params(limit=SMALL_LIMIT),
        cost_estimate=pl.CostEstimate(
            flops=4 * slots * depth * ff,
            bytes_accessed=4 * experts * depth * ff + 4 * slots * ff,
            transcendentals=0,
        ),
        name="gate_up",
    )(x, perm, gain, gate_proj, up_proj)


def activate_kernel(x_ref, out_ref):
    ff = out_ref.shape[1]
    rows = out_ref.shape[0]
    parts = x_ref.shape[0]
    squares = jnp.zeros((rows, 1), jnp.float32)
    for part in range(parts):
        pad = x_ref[part, :, 2 * ff :].astype(jnp.float32)
        squares = squares + pad[:, 0:1] + pad[:, 1:2]
    inv_rms = lax.rsqrt(squares / D + EPSILON)
    step = 256
    for at in range(0, ff, step):
        gate = jnp.zeros((rows, step), jnp.float32)
        up = jnp.zeros((rows, step), jnp.float32)
        for part in range(parts):
            gate = gate + x_ref[part, :, at : at + step].astype(jnp.float32)
            up = up + x_ref[part, :, ff + at : ff + at + step].astype(jnp.float32)
        gate = gate * inv_rms
        up = up * inv_rms
        out_ref[:, at : at + step] = (gate / (1.0 + jnp.exp(-gate)) * up).astype(jnp.bfloat16)


def activate(parts):
    _, rows, width = parts.shape
    return pl.pallas_call(
        activate_kernel,
        out_shape=jax.ShapeDtypeStruct((rows, (width - LANES) // 2), jnp.bfloat16),
        compiler_params=params(limit=SMALL_LIMIT),
        name="activate",
    )(parts)


def down_kernel(act_ref, back_ref, down_ref, out_ref, all_ref):
    experts = down_ref.shape[0]
    count = act_ref.shape[0] // experts
    for e in range(experts):
        at = slice(e * count, (e + 1) * count)
        all_ref[at, :] = jnp.dot(
            act_ref[at, :], down_ref[e], preferred_element_type=jnp.float32
        ).astype(jnp.bfloat16)
    out_ref[...] = jnp.dot(
        back_ref[...], all_ref[...], preferred_element_type=jnp.float32
    ).astype(jnp.bfloat16)


def down(act, back, down_proj):
    experts, ff, width = down_proj.shape
    slots = act.shape[0]
    vmem = pl.BlockSpec(memory_space=pltpu.VMEM)
    return pl.pallas_call(
        down_kernel,
        in_specs=[vmem] * 3,
        out_specs=vmem,
        out_shape=jax.ShapeDtypeStruct((slots, width), jnp.bfloat16),
        scratch_shapes=[pltpu.VMEM((slots, width), jnp.bfloat16)],
        compiler_params=params(limit=SMALL_LIMIT),
        cost_estimate=pl.CostEstimate(
            flops=2 * slots * ff * width,
            bytes_accessed=2 * experts * ff * width,
            transcendentals=0,
        ),
        name="down",
    )(act, back, down_proj)


def per_device(
    queries,
    tree_key_cache,
    tree_value_cache,
    tree_mask,
    lengths,
    out_weight,
    residual,
    norm_gain,
    expert_ids,
    gate_weights,
    gate_proj,
    up_proj,
    down_proj,
):
    rows = queries.shape[0]
    blocks, part_tokens = tree_key_cache.shape[:2]
    n_blk = lax.axis_size(BLK)
    n_narrow = lax.axis_size(NARROW)
    zl, x, core = (lax.axis_index(name) for name in BLK)
    zh, yh, yl = (lax.axis_index(name) for name in NARROW)
    kv_head = zh * 2 + yl
    heads = QUERY_HEADS // n_narrow
    width = heads * HEAD_SIZE
    swap = [(0, 1), (1, 0)]
    size_x = lax.axis_size("x")

    kv = jnp.stack([tree_key_cache, tree_value_cache])
    kv = kv.reshape(2, blocks, part_tokens, KEY_VALUE_HEADS, HEAD_SIZE).transpose(3, 0, 1, 2, 4)
    own_kv = [lax.dynamic_index_in_dim(kv, kv_head, 0, False)]
    for step in range(1, KEY_VALUE_HEADS):
        piece = lax.dynamic_index_in_dim(kv, kv_head ^ step, 0, False)
        pairs = [(i, i ^ step) for i in range(KEY_VALUE_HEADS)]
        own_kv.append(lax.ppermute(piece, ("zh", "yl"), pairs))
    kv = own_kv + [lax.ppermute(piece, "core", swap) for piece in own_kv]

    both = lax.dynamic_slice_in_dim(queries, kv_head * 2 * width, 2 * width, 1)
    extra = jnp.concatenate(
        [
            tree_mask.astype(jnp.bfloat16),
            (lengths // 256).astype(jnp.bfloat16)[:, None],
            (lengths % 256).astype(jnp.bfloat16)[:, None],
            jnp.zeros((rows, LANES - TREE_BLOCKS - 2), jnp.bfloat16),
        ],
        axis=1,
    )
    own_q = lax.dynamic_slice_in_dim(both, core * width, width, 1)
    other_q = lax.dynamic_slice_in_dim(both, (1 - core) * width, width, 1)
    own_q = jnp.concatenate([own_q, extra], axis=1)
    other_q = lax.ppermute(jnp.concatenate([other_q, extra], axis=1), "core", swap)
    pair = jnp.concatenate([own_q, other_q], axis=0)
    all_q, groups = [], []
    for dx in range(size_x):
        for dz in range(2):
            pairs = [
                (z * size_x + i, (z ^ dz) * size_x + (i + dx) % size_x)
                for z in range(2)
                for i in range(size_x)
            ]
            all_q.append(lax.ppermute(pair, ("zl", "x"), pairs) if dx + dz else pair)
            origin = (zl ^ dz) * size_x + (x - dx) % size_x
            groups += [origin * 2 + core, origin * 2 + (1 - core)]
    sources = [((kv_head ^ s) // 2) * 4 + (kv_head ^ s) % 2 for s in range(KEY_VALUE_HEADS)]
    zero = jnp.int32(0)
    info = [zl * size_x + x, core, yh, zero] + sources + groups
    info = jnp.stack([value.astype(jnp.int32) for value in info])
    group_axes = ("zl", "x", "yh")
    attended = []
    for half in range(2):
        partial = attention(info, all_q, kv, half * (heads // 2), heads // 2)
        partial = lax.all_to_all(partial.reshape(n_blk, rows, -1), group_axes, 0, 0)
        attended.append(combine(partial, heads // 2))

    mine = jnp.where(core == 0, attended[0], attended[1])
    other = jnp.where(core == 0, attended[1], attended[0])
    other = lax.ppermute(other, "core", swap)
    first = jnp.where(core == 0, mine, other)
    second = jnp.where(core == 0, other, mine)
    attended = jnp.stack([first, second])
    gathered = jnp.zeros((KEY_VALUE_HEADS,) + attended.shape, attended.dtype)
    gathered = lax.dynamic_update_index_in_dim(gathered, attended, kv_head, 0)
    for step in range(1, KEY_VALUE_HEADS):
        pairs = [(i, i ^ step) for i in range(KEY_VALUE_HEADS)]
        piece = lax.ppermute(attended, ("zh", "yl"), pairs)
        gathered = lax.dynamic_update_index_in_dim(gathered, piece, kv_head ^ step, 0)
    gathered = gathered.reshape(n_blk // 2, 1, rows, -1)
    gathered = jnp.broadcast_to(gathered, (n_blk // 2, 2) + gathered.shape[2:])
    gathered = lax.all_to_all(gathered.reshape((n_blk,) + gathered.shape[2:]), group_axes, 0, 0)
    projected = jnp.dot(
        gathered.reshape(n_blk * rows, -1), out_weight, preferred_element_type=jnp.float32
    )
    projected = projected.reshape(n_blk // 2, 2, rows, -1)
    mine = lax.dynamic_index_in_dim(projected, core, 1, False)
    other = lax.dynamic_index_in_dim(projected, 1 - core, 1, False).astype(jnp.bfloat16)
    projected = (mine + lax.ppermute(other, "core", swap).astype(jnp.float32)).astype(jnp.bfloat16)
    projected = lax.all_to_all(projected, ("zl", "x"), 0, 0)
    projected = jnp.sum(projected.astype(jnp.float32), axis=0)
    hidden_b = (residual.astype(jnp.float32) + projected).astype(jnp.bfloat16)

    exp_dev = gate_proj.shape[0]
    n_experts = exp_dev * n_blk
    flat_ids = expert_ids.reshape(-1)
    expert_hot = (flat_ids[:, None] == jnp.arange(n_experts)[None, :]).astype(jnp.int32)
    earlier = jnp.cumsum(expert_hot, axis=0) - expert_hot
    slot_of = jnp.sum(earlier * expert_hot, axis=1)
    target = (flat_ids * CAP + slot_of).reshape(rows, TOP)
    slots = n_experts * CAP
    at_slot = target[:, :, None] == jnp.arange(slots)[None, None, :]
    select = jnp.any(at_slot, axis=1).astype(jnp.bfloat16)
    mixing = jnp.sum(jnp.where(at_slot, gate_weights[:, :, None], 0.0), axis=1)
    outgoing = lax.dot_general(
        select, hidden_b, (((0,), (0,)), ((), ())), preferred_element_type=jnp.float32
    ).astype(jnp.bfloat16)
    incoming = lax.all_to_all(outgoing.reshape(n_blk, exp_dev * CAP, -1), BLK, 0, 0)

    place = jnp.arange(slots)
    expert, rest = place // (n_blk * CAP), place % (n_blk * CAP)
    order = (rest // CAP) * (exp_dev * CAP) + expert * CAP + rest % CAP
    perm = (order[:, None] == place[None, :]).astype(jnp.bfloat16)

    back = (place[:, None] == order[None, :]).astype(jnp.bfloat16)
    sums = gate_up(
        incoming.reshape(slots, -1), perm, norm_gain.reshape(1, -1), gate_proj, up_proj
    )
    sums = lax.all_to_all(sums.reshape(n_narrow, slots // n_narrow, -1), NARROW, 0, 0)
    activated = gather_by_exchange(activate(sums), NARROW).reshape(slots, -1)
    expert_out = down(activated, back, down_proj)
    returned = lax.all_to_all(expert_out.reshape(n_blk, exp_dev * CAP, -1), BLK, 0, 0)
    returned = returned.reshape(slots, -1)
    mix_high = lax.reduce_precision(mixing, 8, 7)
    mix_low = mixing - mix_high
    mixed_in = jnp.dot(
        mix_high.astype(jnp.bfloat16), returned, preferred_element_type=jnp.float32
    ) + jnp.dot(mix_low.astype(jnp.bfloat16), returned, preferred_element_type=jnp.float32)
    return (hidden_b.astype(jnp.float32) + mixed_in).astype(jnp.bfloat16)


def solution(mesh):
    shape = (2, 4, 2, 2, 2, 2)
    fine = Mesh(mesh.devices.reshape(shape), BLK + NARROW)
    in_specs = (
        P(BLK, None),
        P(BLK, NARROW, None),
        P(BLK, NARROW, None),
        P(BLK, None),
        P(BLK),
        P(BLK, NARROW),
        P(BLK, NARROW),
        P(NARROW),
        P(BLK, None),
        P(BLK, None),
        P(BLK, NARROW, None),
        P(BLK, NARROW, None),
        P(BLK, None, NARROW),
    )
    out_specs = P(BLK, NARROW)
    return jax.shard_map(
        per_device, mesh=fine, in_specs=in_specs, out_specs=out_specs, check_vma=False
    )
```

```python
import functools

import jax
import jax.numpy as jnp
from jax import lax
from jax.experimental import pallas as pl
from jax.experimental.pallas import tpu as pltpu
from jax.sharding import Mesh
from jax.sharding import PartitionSpec as P

D = 4096
QUERY_HEADS = 64
KEY_VALUE_HEADS = 4
HEAD_SIZE = 128
FF = 1536
TOP = 8
CAP = 6
BLOCK_TOKENS = 1024
TREE_BLOCKS = 64
NEGATIVE_FILLER = -1e30
EPSILON = 1e-06
SCORE_SCALE = HEAD_SIZE ** (-0.5)
LOG2E = 1.4426950408889634
LANES = 128
BLK = ("zl", "x", "core")
NARROW = ("zh", "yh", "yl")
SAFE_POWER = 60.0
VMEM_LIMIT = 40 * 1024 * 1024
LARGE_LIMIT = 56 * 1024 * 1024
SMALL_LIMIT = 12 * 1024 * 1024


def params(limit):
    return pltpu.CompilerParams(vmem_limit_bytes=limit)


def split_bf16(value):
    high = value.astype(jnp.bfloat16)
    rest = value - high.astype(jnp.float32)
    mid = rest.astype(jnp.bfloat16)
    low = (rest - mid.astype(jnp.float32)).astype(jnp.bfloat16)
    return high, mid, low


def attention_kernel(heads, info_ref, *refs):
    q_in = refs[0:4]
    kv_in = refs[4:12]
    out_ref, q_ref, k_ref, v_ref, vt_ref, lim_ref, mask_ref, s_ref, lse_ref, sem = refs[12:]
    rows = q_ref.shape[0]
    base = heads * HEAD_SIZE
    chip, core = info_ref[0], info_ref[1]
    chip_blocks, sources = k_ref.shape[:2]
    blocks = chip_blocks // 2
    span = sources * LANES
    tokens = chip_blocks * span
    step = rows // len(q_in)
    factor = SCORE_SCALE * LOG2E

    copies = []
    for i, ref in enumerate(q_in):
        at = pl.ds(i * step, step)
        copies.append(pltpu.make_async_copy(ref, q_ref.at[at], sem.at[len(copies)]))
    for i, ref in enumerate(kv_in):
        side, s = i // sources, i % sources
        for part, target in enumerate((k_ref, v_ref)):
            to = target.at[pl.ds(side * blocks, blocks), s]
            copies.append(pltpu.make_async_copy(ref.at[part], to, sem.at[len(copies)]))
    for copy in copies:
        copy.start()
    for copy in copies:
        copy.wait()

    extra = q_ref[:, base:].astype(jnp.float32).T
    lim_ref[...] = extra
    length = extra[TREE_BLOCKS : TREE_BLOCKS + 1] * 256.0 + extra[TREE_BLOCKS + 1 : TREE_BLOCKS + 2]
    first = pl.multiple_of(chip * chip_blocks, chip_blocks)
    reads = lim_ref[pl.ds(first, chip_blocks), :]
    block_id = lax.broadcasted_iota(jnp.int32, (chip_blocks, rows), 0) + first
    bound = length - (block_id * BLOCK_TOKENS).astype(jnp.float32)
    lim_ref[0:chip_blocks, :] = jnp.where(reads > 0.5, bound, 0.0)
    token = lax.broadcasted_iota(jnp.int32, (LANES, 1), 0)
    token = [
        (token + info_ref[4 + s] * LANES).astype(jnp.float32) for s in range(sources)
    ]
    token = jnp.concatenate(token, axis=0)
    sub = lax.broadcasted_iota(jnp.int32, (16, tokens), 0)
    vt_ref[HEAD_SIZE:, :] = jnp.where(sub == 0, 1.0, 0.0).astype(jnp.bfloat16)
    most_k = jnp.zeros((LANES, 1), jnp.float32)
    for i in range(chip_blocks):
        at = slice(i * span, (i + 1) * span)
        vt_ref[:HEAD_SIZE, at] = v_ref[i].reshape(span, HEAD_SIZE).T
        side = core if i < blocks else 1 - core
        lim = lim_ref[pl.ds(side * blocks + i % blocks, 1), :]
        mask_ref[at, :] = jnp.where(token < lim, 1.0, 0.0).astype(jnp.bfloat16)
        for s in range(sources):
            keys = k_ref[i, s].astype(jnp.float32)
            most_k = jnp.maximum(most_k, jnp.sum(keys * keys, axis=1, keepdims=True))
    most_q = jnp.zeros((rows, 1), jnp.float32)
    for h in range(heads):
        q = q_ref[:, h * HEAD_SIZE : (h + 1) * HEAD_SIZE].astype(jnp.float32)
        most_q = jnp.maximum(most_q, jnp.sum(q * q, axis=1, keepdims=True))
    most = jnp.max(most_q) * jnp.max(most_k) * (factor * factor)
    small = most <= SAFE_POWER * SAFE_POWER

    def finish(h, cols, acc, top):
        total = acc[HEAD_SIZE : HEAD_SIZE + 1]
        some = total > 0
        safe = jnp.where(some, total, 1.0)
        result = (acc[:HEAD_SIZE] / safe).astype(jnp.bfloat16).T
        group = rows // 16
        for i in range(16):
            row = pl.multiple_of(info_ref[8 + i] * group, group)
            out_ref[pl.ds(row, group), cols] = result[i * group : (i + 1) * group]
        lse = jnp.where(some, top * SCORE_SCALE + jnp.log(safe), NEGATIVE_FILLER)
        lse_ref[pl.ds(h, 1), :] = lse

    def head_columns(h):
        return pl.ds(pl.multiple_of(h * HEAD_SIZE, HEAD_SIZE), HEAD_SIZE)

    chunk = 2

    def small_head(h, carry):
        cols = head_columns(h)
        qt = q_ref[:, cols].T
        acc = jnp.zeros((HEAD_SIZE + 16, rows), jnp.float32)
        for i in range(0, chip_blocks, chunk):
            at = slice(i * span, (i + chunk) * span)
            keys = k_ref[i : i + chunk].reshape(chunk * span, HEAD_SIZE)
            s = jnp.dot(keys, qt, preferred_element_type=jnp.float32) * factor
            p = jnp.exp2(s).astype(jnp.bfloat16) * mask_ref[at, :]
            acc = acc + jnp.dot(vt_ref[:, at], p, preferred_element_type=jnp.float32)
        finish(h, cols, acc, 0.0)
        return carry

    def any_head(h, carry):
        cols = head_columns(h)
        qt = q_ref[:, cols].T
        top = jnp.full((1, rows), -1e29, jnp.float32)
        for i in range(chip_blocks):
            at = slice(i * span, (i + 1) * span)
            keys = k_ref[i].reshape(span, HEAD_SIZE)
            s = jnp.dot(keys, qt, preferred_element_type=jnp.float32)
            s = jnp.where(mask_ref[at, :].astype(jnp.float32) > 0.5, s, NEGATIVE_FILLER)
            s_ref[at, :] = s
            top = jnp.maximum(top, jnp.max(s, axis=0, keepdims=True))
        acc = jnp.zeros((HEAD_SIZE + 16, rows), jnp.float32)
        for i in range(chip_blocks):
            at = slice(i * span, (i + 1) * span)
            p = jnp.exp2((s_ref[at, :] - top) * factor).astype(jnp.bfloat16)
            acc = acc + jnp.dot(vt_ref[:, at], p, preferred_element_type=jnp.float32)
        finish(h, cols, acc, top)
        return carry

    @pl.when(small)
    def _():
        lax.fori_loop(0, heads, small_head, 0)

    @pl.when(jnp.logical_not(small))
    def _():
        lax.fori_loop(0, heads, any_head, 0)

    high, mid, low = split_bf16(lse_ref[...])
    pieces = [piece.astype(jnp.float32) for piece in (high, mid, low)]
    pieces.append(jnp.zeros((LANES - 3 * heads, rows), jnp.float32))
    result = jnp.concatenate(pieces, axis=0).T.astype(jnp.bfloat16)
    group = rows // 16
    for i in range(16):
        row = pl.multiple_of(info_ref[8 + i] * group, group)
        out_ref[pl.ds(row, group), base:] = result[i * group : (i + 1) * group]


def attention(info, queries, kv):
    step, width = queries[0].shape
    rows = step * len(queries)
    heads = (width - LANES) // HEAD_SIZE
    blocks = kv[0].shape[1]
    sources = len(kv) // 2
    tokens = len(kv) * blocks * LANES
    anywhere = pl.BlockSpec(memory_space=pl.ANY)
    tiles = (2 * blocks, sources, LANES, HEAD_SIZE)
    return pl.pallas_call(
        functools.partial(attention_kernel, heads),
        in_specs=[pl.BlockSpec(memory_space=pltpu.SMEM)] + [anywhere] * (len(queries) + len(kv)),
        out_specs=pl.BlockSpec(memory_space=pltpu.VMEM),
        out_shape=jax.ShapeDtypeStruct((rows, width), jnp.bfloat16),
        scratch_shapes=[
            pltpu.VMEM((rows, width), jnp.bfloat16),
            pltpu.VMEM(tiles, jnp.bfloat16),
            pltpu.VMEM(tiles, jnp.bfloat16),
            pltpu.VMEM((HEAD_SIZE + 16, tokens), jnp.bfloat16),
            pltpu.VMEM((LANES, rows), jnp.float32),
            pltpu.VMEM((tokens, rows), jnp.bfloat16),
            pltpu.VMEM((tokens, rows), jnp.float32),
            pltpu.VMEM((heads, rows), jnp.float32),
            pltpu.SemaphoreType.DMA((len(queries) + 2 * len(kv),)),
        ],
        compiler_params=params(limit=VMEM_LIMIT),
        cost_estimate=pl.CostEstimate(
            flops=6 * rows * heads * tokens * HEAD_SIZE,
            bytes_accessed=6 << 20,
            transcendentals=rows * heads * tokens,
        ),
        name="attention",
    )(info, *queries, *kv)


def combine_kernel(heads, x_ref, out_ref):
    base = heads * HEAD_SIZE
    info = x_ref[:, :, base:].astype(jnp.float32)
    for h in range(heads):
        lse = info[:, :, h : h + 1] + info[:, :, 8 + h : 9 + h]
        lse = lse + info[:, :, 16 + h : 17 + h]
        scale = jnp.exp(lse - jnp.max(lse, axis=0, keepdims=True))
        cols = slice(h * HEAD_SIZE, (h + 1) * HEAD_SIZE)
        acc = jnp.sum(x_ref[:, :, cols].astype(jnp.float32) * scale, axis=0)
        out_ref[:, cols] = (acc / jnp.sum(scale, axis=0)).astype(jnp.bfloat16)


def combine(parts, heads):
    _, rows, _ = parts.shape
    return pl.pallas_call(
        functools.partial(combine_kernel, heads),
        out_shape=jax.ShapeDtypeStruct((rows, heads * HEAD_SIZE), jnp.bfloat16),
        compiler_params=params(limit=SMALL_LIMIT),
        cost_estimate=pl.CostEstimate(
            flops=4 * parts.size, bytes_accessed=2 * parts.size, transcendentals=0
        ),
        name="combine",
    )(parts)


def gate_up_kernel(x_ref, perm_ref, gain_ref, gate_hbm, up_hbm, out_ref, gate_ref, up_ref, sem):
    experts, _, width = gate_ref.shape
    count = x_ref.shape[0] // experts
    copies = [
        [
            pltpu.make_async_copy(gate_hbm.at[e], gate_ref.at[e], sem.at[0, e]),
            pltpu.make_async_copy(up_hbm.at[e], up_ref.at[e], sem.at[1, e]),
        ]
        for e in range(experts)
    ]
    for pair in copies:
        for copy in pair:
            copy.start()
    for e in range(experts):
        at = slice(e * count, (e + 1) * count)
        rows = jnp.dot(perm_ref[at, :], x_ref[...], preferred_element_type=jnp.float32)
        scaled = (rows * gain_ref[...]).astype(jnp.bfloat16)
        squares = jnp.sum(rows * rows, axis=1, keepdims=True)
        high, mid, _ = split_bf16(squares)
        lane = lax.broadcasted_iota(jnp.int32, (count, LANES), 1)
        pad = jnp.where(lane == 0, high.astype(jnp.float32), 0.0)
        pad = jnp.where(lane == 1, mid.astype(jnp.float32), pad)
        out_ref[at, 2 * width :] = pad.astype(jnp.bfloat16)
        copies[e][0].wait()
        out_ref[at, :width] = jnp.dot(
            scaled, gate_ref[e], preferred_element_type=jnp.float32
        ).astype(jnp.bfloat16)
        copies[e][1].wait()
        out_ref[at, width : 2 * width] = jnp.dot(
            scaled, up_ref[e], preferred_element_type=jnp.float32
        ).astype(jnp.bfloat16)


def gate_up(x, perm, gain, gate_proj, up_proj):
    experts, depth, ff = gate_proj.shape
    slots = x.shape[0]
    vmem = pl.BlockSpec(memory_space=pltpu.VMEM)
    anywhere = pl.BlockSpec(memory_space=pl.ANY)
    return pl.pallas_call(
        gate_up_kernel,
        in_specs=[vmem] * 3 + [anywhere] * 2,
        out_specs=vmem,
        out_shape=jax.ShapeDtypeStruct((slots, 2 * ff + LANES), jnp.bfloat16),
        scratch_shapes=[
            pltpu.VMEM(gate_proj.shape, jnp.bfloat16),
            pltpu.VMEM(up_proj.shape, jnp.bfloat16),
            pltpu.SemaphoreType.DMA((2, experts)),
        ],
        compiler_params=params(limit=LARGE_LIMIT),
        cost_estimate=pl.CostEstimate(
            flops=4 * slots * depth * ff,
            bytes_accessed=4 * experts * depth * ff + 4 * slots * ff,
            transcendentals=0,
        ),
        name="gate_up",
    )(x, perm, gain, gate_proj, up_proj)


def activate_kernel(x_ref, out_ref):
    parts, rows, ff = out_ref.shape
    squares = jnp.zeros((rows, 1), jnp.float32)
    for part in range(parts):
        pad = x_ref[part, :, 2 * ff :].astype(jnp.float32)
        squares = squares + pad[:, 0:1] + pad[:, 1:2]
    inv_rms = lax.rsqrt(squares / D + EPSILON)
    step = 256
    for at in range(0, ff, step):
        gate = jnp.zeros((rows, step), jnp.float32)
        up = jnp.zeros((rows, step), jnp.float32)
        for part in range(parts):
            gate = gate + x_ref[part, :, at : at + step].astype(jnp.float32)
            up = up + x_ref[part, :, ff + at : ff + at + step].astype(jnp.float32)
        gate = gate * inv_rms
        up = up * inv_rms
        result = (gate / (1.0 + jnp.exp(-gate)) * up).astype(jnp.bfloat16)
        for part in range(parts):
            out_ref[part, :, at : at + step] = result


def activate(parts):
    count, rows, width = parts.shape
    return pl.pallas_call(
        activate_kernel,
        out_shape=jax.ShapeDtypeStruct((count, rows, (width - LANES) // 2), jnp.bfloat16),
        compiler_params=params(limit=SMALL_LIMIT),
        name="activate",
    )(parts)


def down_kernel(act_ref, back_ref, down_hbm, out_ref, all_ref, down_ref, sem):
    experts = down_ref.shape[0]
    count = act_ref.shape[0] // experts
    copies = [
        pltpu.make_async_copy(down_hbm.at[e], down_ref.at[e], sem.at[e]) for e in range(experts)
    ]
    for copy in copies:
        copy.start()
    for e in range(experts):
        at = slice(e * count, (e + 1) * count)
        copies[e].wait()
        all_ref[at, :] = jnp.dot(
            act_ref[at, :], down_ref[e], preferred_element_type=jnp.float32
        ).astype(jnp.bfloat16)
    out_ref[...] = jnp.dot(
        back_ref[...], all_ref[...], preferred_element_type=jnp.float32
    ).astype(jnp.bfloat16)


def down(act, back, down_proj):
    experts, ff, width = down_proj.shape
    slots = act.shape[0]
    vmem = pl.BlockSpec(memory_space=pltpu.VMEM)
    return pl.pallas_call(
        down_kernel,
        in_specs=[vmem] * 2 + [pl.BlockSpec(memory_space=pl.ANY)],
        out_specs=vmem,
        out_shape=jax.ShapeDtypeStruct((slots, width), jnp.bfloat16),
        scratch_shapes=[
            pltpu.VMEM((slots, width), jnp.bfloat16),
            pltpu.VMEM(down_proj.shape, jnp.bfloat16),
            pltpu.SemaphoreType.DMA((experts,)),
        ],
        compiler_params=params(limit=LARGE_LIMIT),
        cost_estimate=pl.CostEstimate(
            flops=2 * slots * ff * width,
            bytes_accessed=2 * experts * ff * width,
            transcendentals=0,
        ),
        name="down",
    )(act, back, down_proj)


def per_device(
    queries,
    tree_key_cache,
    tree_value_cache,
    tree_mask,
    lengths,
    out_weight,
    residual,
    norm_gain,
    expert_ids,
    gate_weights,
    gate_proj,
    up_proj,
    down_proj,
):
    rows = queries.shape[0]
    blocks, part_tokens = tree_key_cache.shape[:2]
    n_blk = lax.axis_size(BLK)
    n_narrow = lax.axis_size(NARROW)
    zl, x, core = (lax.axis_index(name) for name in BLK)
    zh, yh, yl = (lax.axis_index(name) for name in NARROW)
    kv_head = yh * 2 + yl
    heads = QUERY_HEADS // n_narrow
    width = heads * HEAD_SIZE
    swap = [(0, 1), (1, 0)]
    size_x = lax.axis_size("x")

    both = lax.dynamic_slice_in_dim(queries, kv_head * 2 * width, 2 * width, 1)
    extra = jnp.concatenate(
        [
            tree_mask.astype(jnp.bfloat16),
            (lengths // 256).astype(jnp.bfloat16)[:, None],
            (lengths % 256).astype(jnp.bfloat16)[:, None],
            jnp.zeros((rows, LANES - TREE_BLOCKS - 2), jnp.bfloat16),
        ],
        axis=1,
    )
    own_q = lax.dynamic_slice_in_dim(both, core * width, width, 1)
    other_q = lax.dynamic_slice_in_dim(both, (1 - core) * width, width, 1)
    own_q = jnp.concatenate([own_q, extra], axis=1)
    other_q = lax.ppermute(jnp.concatenate([other_q, extra], axis=1), "core", swap)
    pair = jnp.concatenate([own_q, other_q], axis=0)
    pair = jnp.concatenate([pair, lax.ppermute(pair, "zl", swap)], axis=0)

    def head_piece(head):
        at = head * HEAD_SIZE
        return jnp.stack(
            [
                lax.dynamic_slice_in_dim(cache, at, HEAD_SIZE, 2) + other_q[0, 0] * 0
                for cache in (tree_key_cache, tree_value_cache)
            ]
        )

    kv = [head_piece(kv_head)]
    for step in range(1, KEY_VALUE_HEADS):
        pairs = [(i, i ^ step) for i in range(KEY_VALUE_HEADS)]
        kv.append(lax.ppermute(head_piece(kv_head ^ step), ("yh", "yl"), pairs))
    kv = kv + [lax.ppermute(piece, "core", swap) for piece in kv]
    sources = [zh * KEY_VALUE_HEADS + (kv_head ^ s) for s in range(KEY_VALUE_HEADS)]

    all_q, groups = [pair], []
    for dx in range(size_x):
        if dx:
            pairs = [(i, (i + dx) % size_x) for i in range(size_x)]
            all_q.append(lax.ppermute(pair, "x", pairs))
        for dz in range(2):
            origin = (zl ^ dz) * size_x + (x - dx) % size_x
            groups += [origin * 2 + core, origin * 2 + (1 - core)]
    zero = jnp.int32(0)
    info = [zl * size_x + x, core, zero, zero] + sources + groups
    info = jnp.stack([value.astype(jnp.int32) for value in info])
    group_axes = ("zl", "x", "zh")
    partial = attention(info, all_q, kv)
    partial = lax.all_to_all(partial.reshape(n_blk, rows, width + LANES), group_axes, 0, 0)
    attended = combine(partial, heads)
    attended = [attended[:, : width // 2], attended[:, width // 2 :]]

    mine = jnp.where(core == 0, attended[0], attended[1])
    other = jnp.where(core == 0, attended[1], attended[0])
    other = lax.ppermute(other, "core", swap)
    first = jnp.where(core == 0, mine, other)
    second = jnp.where(core == 0, other, mine)
    attended = jnp.stack([first, second])
    gathered = jnp.zeros((KEY_VALUE_HEADS,) + attended.shape, attended.dtype)
    gathered = lax.dynamic_update_index_in_dim(gathered, attended, kv_head, 0)
    for step in range(1, KEY_VALUE_HEADS):
        pairs = [(i, i ^ step) for i in range(KEY_VALUE_HEADS)]
        piece = lax.ppermute(attended, ("yh", "yl"), pairs)
        gathered = lax.dynamic_update_index_in_dim(gathered, piece, kv_head ^ step, 0)
    gathered = gathered.reshape(n_blk // 2, 1, rows, -1)
    gathered = jnp.broadcast_to(gathered, (n_blk // 2, 2) + gathered.shape[2:])
    gathered = lax.all_to_all(gathered.reshape((n_blk,) + gathered.shape[2:]), group_axes, 0, 0)
    projected = jnp.dot(
        gathered.reshape(n_blk * rows, -1), out_weight, preferred_element_type=jnp.float32
    )
    projected = projected.reshape(n_blk // 2, 2, rows, -1)
    mine = lax.dynamic_index_in_dim(projected, core, 1, False)
    other = lax.dynamic_index_in_dim(projected, 1 - core, 1, False).astype(jnp.bfloat16)
    projected = (mine + lax.ppermute(other, "core", swap).astype(jnp.float32)).astype(jnp.bfloat16)
    projected = lax.all_to_all(projected, ("zl", "x"), 0, 0)
    projected = jnp.sum(projected.astype(jnp.float32), axis=0)
    hidden_b = (residual.astype(jnp.float32) + projected).astype(jnp.bfloat16)

    exp_dev = gate_proj.shape[0]
    n_experts = exp_dev * n_blk
    flat_ids = expert_ids.reshape(-1)
    expert_hot = (flat_ids[:, None] == jnp.arange(n_experts)[None, :]).astype(jnp.int32)
    earlier = jnp.cumsum(expert_hot, axis=0) - expert_hot
    slot_of = jnp.sum(earlier * expert_hot, axis=1)
    target = (flat_ids * CAP + slot_of).reshape(rows, TOP)
    slots = n_experts * CAP
    at_slot = target[:, :, None] == jnp.arange(slots)[None, None, :]
    select = jnp.any(at_slot, axis=1).astype(jnp.bfloat16)
    mixing = jnp.sum(jnp.where(at_slot, gate_weights[:, :, None], 0.0), axis=1)
    outgoing = lax.dot_general(
        select, hidden_b, (((0,), (0,)), ((), ())), preferred_element_type=jnp.float32
    ).astype(jnp.bfloat16)
    incoming = lax.all_to_all(outgoing.reshape(n_blk, exp_dev * CAP, -1), BLK, 0, 0)

    place = jnp.arange(slots)
    expert, rest = place // (n_blk * CAP), place % (n_blk * CAP)
    order = (rest // CAP) * (exp_dev * CAP) + expert * CAP + rest % CAP
    perm = (order[:, None] == place[None, :]).astype(jnp.bfloat16)

    back = (place[:, None] == order[None, :]).astype(jnp.bfloat16)
    sums = gate_up(
        incoming.reshape(slots, -1), perm, norm_gain.reshape(1, -1), gate_proj, up_proj
    )
    sums = lax.all_to_all(sums.reshape(n_narrow, slots // n_narrow, -1), NARROW, 0, 0)
    activated = activate(sums)
    activated = lax.all_to_all(activated, NARROW, 0, 0).reshape(slots, -1)
    expert_out = down(activated, back, down_proj)
    returned = lax.all_to_all(expert_out.reshape(n_blk, exp_dev * CAP, -1), BLK, 0, 0)
    returned = returned.reshape(slots, -1)
    mix_high = lax.reduce_precision(mixing, 8, 7)
    mix_low = mixing - mix_high
    mixed_in = jnp.dot(
        mix_high.astype(jnp.bfloat16), returned, preferred_element_type=jnp.float32
    ) + jnp.dot(mix_low.astype(jnp.bfloat16), returned, preferred_element_type=jnp.float32)
    return (hidden_b.astype(jnp.float32) + mixed_in).astype(jnp.bfloat16)


def solution(mesh):
    shape = (2, 4, 2, 2, 2, 2)
    fine = Mesh(mesh.devices.reshape(shape), BLK + NARROW)
    in_specs = (
        P(BLK, None),
        P(BLK, NARROW, None),
        P(BLK, NARROW, None),
        P(BLK, None),
        P(BLK),
        P(BLK, NARROW),
        P(BLK, NARROW),
        P(NARROW),
        P(BLK, None),
        P(BLK, None),
        P(BLK, NARROW, None),
        P(BLK, NARROW, None),
        P(BLK, None, NARROW),
    )
    out_specs = P(BLK, NARROW)
    return jax.shard_map(
        per_device, mesh=fine, in_specs=in_specs, out_specs=out_specs, check_vma=False
    )
```

```python
import functools

import jax
import jax.numpy as jnp
from jax import lax
from jax.experimental import pallas as pl
from jax.experimental.pallas import tpu as pltpu
from jax.sharding import Mesh
from jax.sharding import PartitionSpec as P

D = 4096
QUERY_HEADS = 64
KEY_VALUE_HEADS = 4
HEAD_SIZE = 128
FF = 1536
TOP = 8
CAP = 6
BLOCK_TOKENS = 1024
TREE_BLOCKS = 64
NEGATIVE_FILLER = -1e30
EPSILON = 1e-06
SCORE_SCALE = HEAD_SIZE ** (-0.5)
LOG2E = 1.4426950408889634
LANES = 128
BLK = ("zl", "x", "core")
NARROW = ("zh", "yh", "yl")
SAFE_POWER = 100.0
VMEM_LIMIT = 40 * 1024 * 1024
LARGE_LIMIT = 56 * 1024 * 1024
SMALL_LIMIT = 12 * 1024 * 1024


def params(limit):
    return pltpu.CompilerParams(vmem_limit_bytes=limit)


def split_bf16(value):
    high = value.astype(jnp.bfloat16)
    rest = value - high.astype(jnp.float32)
    mid = rest.astype(jnp.bfloat16)
    low = (rest - mid.astype(jnp.float32)).astype(jnp.bfloat16)
    return high, mid, low


def attention_kernel(heads, info_ref, *refs):
    q_in = refs[0:4]
    kv_in = refs[4:12]
    out_ref, q_ref, k_ref, v_ref, vt_ref, lim_ref, mask_ref, s_ref, lse_ref, sem = refs[12:]
    rows = q_ref.shape[0]
    base = heads * HEAD_SIZE
    chip, core = info_ref[0], info_ref[1]
    chip_blocks, sources = k_ref.shape[:2]
    blocks = chip_blocks // 2
    span = sources * LANES
    tokens = chip_blocks * span
    step = rows // len(q_in)
    factor = SCORE_SCALE * LOG2E

    copies = []
    for i, ref in enumerate(q_in):
        at = pl.ds(i * step, step)
        copies.append(pltpu.make_async_copy(ref, q_ref.at[at], sem.at[len(copies)]))
    for i, ref in enumerate(kv_in):
        side, s = i // sources, i % sources
        for part, target in enumerate((k_ref, v_ref)):
            to = target.at[pl.ds(side * blocks, blocks), s]
            copies.append(pltpu.make_async_copy(ref.at[part], to, sem.at[len(copies)]))
    for copy in copies:
        copy.start()

    sub = lax.broadcasted_iota(jnp.int32, (16, tokens), 0)
    vt_ref[HEAD_SIZE:, :] = jnp.where(sub == 0, 1.0, 0.0).astype(jnp.bfloat16)
    for copy in copies[: len(q_in)]:
        copy.wait()
    extra = q_ref[:, base:].astype(jnp.float32).T
    lim_ref[...] = extra
    length = extra[TREE_BLOCKS : TREE_BLOCKS + 1] * 256.0 + extra[TREE_BLOCKS + 1 : TREE_BLOCKS + 2]
    first = pl.multiple_of(chip * chip_blocks, chip_blocks)
    reads = lim_ref[pl.ds(first, chip_blocks), :]
    block_id = lax.broadcasted_iota(jnp.int32, (chip_blocks, rows), 0) + first
    bound = length - (block_id * BLOCK_TOKENS).astype(jnp.float32)
    lim_ref[0:chip_blocks, :] = jnp.where(reads > 0.5, bound, 0.0)
    most_q = jnp.zeros((rows, 1), jnp.float32)
    for h in range(heads):
        q = q_ref[:, h * HEAD_SIZE : (h + 1) * HEAD_SIZE].astype(jnp.float32)
        most_q = jnp.maximum(most_q, jnp.sum(q * q, axis=1, keepdims=True))
    token = lax.broadcasted_iota(jnp.int32, (LANES, 1), 0)
    token = [(token + info_ref[4 + s] * LANES).astype(jnp.float32) for s in range(sources)]
    token = jnp.concatenate(token, axis=0)
    for i in range(chip_blocks):
        at = slice(i * span, (i + 1) * span)
        side = core if i < blocks else 1 - core
        lim = lim_ref[pl.ds(side * blocks + i % blocks, 1), :]
        mask_ref[at, :] = jnp.where(token < lim, 1.0, 0.0).astype(jnp.bfloat16)
    for copy in copies[len(q_in) :]:
        copy.wait()
    most_k = jnp.zeros((LANES, HEAD_SIZE), jnp.float32)
    for i in range(chip_blocks):
        vt_ref[:HEAD_SIZE, i * span : (i + 1) * span] = v_ref[i].reshape(span, HEAD_SIZE).T
        for s in range(sources):
            keys = k_ref[i, s].astype(jnp.float32)
            most_k = jnp.maximum(most_k, keys * keys)
    most_k = jnp.sum(jnp.max(most_k, axis=0, keepdims=True), axis=1, keepdims=True)
    most = jnp.max(most_q) * jnp.max(most_k) * (factor * factor)
    small = most <= SAFE_POWER * SAFE_POWER

    def finish(h, cols, acc, top):
        total = acc[HEAD_SIZE : HEAD_SIZE + 1]
        some = total > 0
        safe = jnp.where(some, total, 1.0)
        result = (acc[:HEAD_SIZE] / safe).astype(jnp.bfloat16).T
        group = rows // 16
        for i in range(16):
            row = pl.multiple_of(info_ref[8 + i] * group, group)
            out_ref[pl.ds(row, group), cols] = result[i * group : (i + 1) * group]
        lse = jnp.where(some, top * SCORE_SCALE + jnp.log(safe), NEGATIVE_FILLER)
        lse_ref[pl.ds(h, 1), :] = lse

    def head_columns(h):
        return pl.ds(pl.multiple_of(h * HEAD_SIZE, HEAD_SIZE), HEAD_SIZE)

    chunk = 2

    def small_head(h, carry):
        cols = head_columns(h)
        qt = q_ref[:, cols].T
        acc = jnp.zeros((HEAD_SIZE + 16, rows), jnp.float32)
        for i in range(0, chip_blocks, chunk):
            at = slice(i * span, (i + chunk) * span)
            keys = k_ref[i : i + chunk].reshape(chunk * span, HEAD_SIZE)
            s = jnp.dot(keys, qt, preferred_element_type=jnp.float32) * factor
            p = jnp.exp2(s).astype(jnp.bfloat16) * mask_ref[at, :]
            acc = acc + jnp.dot(vt_ref[:, at], p, preferred_element_type=jnp.float32)
        finish(h, cols, acc, 0.0)
        return carry

    def any_head(h, carry):
        cols = head_columns(h)
        qt = q_ref[:, cols].T
        top = jnp.full((1, rows), -1e29, jnp.float32)
        for i in range(chip_blocks):
            at = slice(i * span, (i + 1) * span)
            keys = k_ref[i].reshape(span, HEAD_SIZE)
            s = jnp.dot(keys, qt, preferred_element_type=jnp.float32)
            s = jnp.where(mask_ref[at, :].astype(jnp.float32) > 0.5, s, NEGATIVE_FILLER)
            s_ref[at, :] = s
            top = jnp.maximum(top, jnp.max(s, axis=0, keepdims=True))
        acc = jnp.zeros((HEAD_SIZE + 16, rows), jnp.float32)
        for i in range(chip_blocks):
            at = slice(i * span, (i + 1) * span)
            p = jnp.exp2((s_ref[at, :] - top) * factor).astype(jnp.bfloat16)
            acc = acc + jnp.dot(vt_ref[:, at], p, preferred_element_type=jnp.float32)
        finish(h, cols, acc, top)
        return carry

    @pl.when(small)
    def _():
        lax.fori_loop(0, heads, small_head, 0)

    @pl.when(jnp.logical_not(small))
    def _():
        lax.fori_loop(0, heads, any_head, 0)

    high, mid, low = split_bf16(lse_ref[...])
    pieces = [piece.astype(jnp.float32) for piece in (high, mid, low)]
    pieces.append(jnp.zeros((LANES - 3 * heads, rows), jnp.float32))
    result = jnp.concatenate(pieces, axis=0).T.astype(jnp.bfloat16)
    group = rows // 16
    for i in range(16):
        row = pl.multiple_of(info_ref[8 + i] * group, group)
        out_ref[pl.ds(row, group), base:] = result[i * group : (i + 1) * group]


def attention(info, queries, kv):
    step, width = queries[0].shape
    rows = step * len(queries)
    heads = (width - LANES) // HEAD_SIZE
    blocks = kv[0].shape[1]
    sources = len(kv) // 2
    tokens = len(kv) * blocks * LANES
    anywhere = pl.BlockSpec(memory_space=pl.ANY)
    tiles = (2 * blocks, sources, LANES, HEAD_SIZE)
    return pl.pallas_call(
        functools.partial(attention_kernel, heads),
        in_specs=[pl.BlockSpec(memory_space=pltpu.SMEM)] + [anywhere] * (len(queries) + len(kv)),
        out_specs=pl.BlockSpec(memory_space=pltpu.VMEM),
        out_shape=jax.ShapeDtypeStruct((rows, width), jnp.bfloat16),
        scratch_shapes=[
            pltpu.VMEM((rows, width), jnp.bfloat16),
            pltpu.VMEM(tiles, jnp.bfloat16),
            pltpu.VMEM(tiles, jnp.bfloat16),
            pltpu.VMEM((HEAD_SIZE + 16, tokens), jnp.bfloat16),
            pltpu.VMEM((LANES, rows), jnp.float32),
            pltpu.VMEM((tokens, rows), jnp.bfloat16),
            pltpu.VMEM((tokens, rows), jnp.float32),
            pltpu.VMEM((heads, rows), jnp.float32),
            pltpu.SemaphoreType.DMA((len(queries) + 2 * len(kv),)),
        ],
        compiler_params=params(limit=VMEM_LIMIT),
        cost_estimate=pl.CostEstimate(
            flops=6 * rows * heads * tokens * HEAD_SIZE,
            bytes_accessed=6 << 20,
            transcendentals=rows * heads * tokens,
        ),
        name="attention",
    )(info, *queries, *kv)


def combine_kernel(heads, x_ref, out_ref):
    base = heads * HEAD_SIZE
    info = x_ref[:, :, base:].astype(jnp.float32)
    for h in range(heads):
        lse = info[:, :, h : h + 1] + info[:, :, 8 + h : 9 + h]
        lse = lse + info[:, :, 16 + h : 17 + h]
        scale = jnp.exp(lse - jnp.max(lse, axis=0, keepdims=True))
        cols = slice(h * HEAD_SIZE, (h + 1) * HEAD_SIZE)
        acc = jnp.sum(x_ref[:, :, cols].astype(jnp.float32) * scale, axis=0)
        at = h % (heads // 2) * HEAD_SIZE
        out_ref[h // (heads // 2), :, at : at + HEAD_SIZE] = (
            acc / jnp.sum(scale, axis=0)
        ).astype(jnp.bfloat16)


def combine(parts, heads):
    _, rows, _ = parts.shape
    return pl.pallas_call(
        functools.partial(combine_kernel, heads),
        out_shape=jax.ShapeDtypeStruct((2, rows, heads * HEAD_SIZE // 2), jnp.bfloat16),
        compiler_params=params(limit=SMALL_LIMIT),
        cost_estimate=pl.CostEstimate(
            flops=4 * parts.size, bytes_accessed=2 * parts.size, transcendentals=0
        ),
        name="combine",
    )(parts)


def project_kernel(core_ref, x_ref, weight_ref, mine_ref, other_ref):
    chips, _, rows, depth = x_ref.shape
    core = core_ref[0]
    for ref, side in ((other_ref, 1 - core), (mine_ref, core)):
        x = x_ref[:, pl.ds(side, 1)].reshape(chips * rows, depth)
        product = jnp.dot(x, weight_ref[...], preferred_element_type=jnp.float32)
        ref[...] = product.astype(ref.dtype)


def project(core, x, weight):
    chips, _, rows, _ = x.shape
    shape = (chips * rows, weight.shape[1])
    vmem = pl.BlockSpec(memory_space=pltpu.VMEM)
    return pl.pallas_call(
        project_kernel,
        in_specs=[pl.BlockSpec(memory_space=pltpu.SMEM), vmem, vmem],
        out_specs=[vmem, vmem],
        out_shape=[
            jax.ShapeDtypeStruct(shape, jnp.float32),
            jax.ShapeDtypeStruct(shape, jnp.bfloat16),
        ],
        compiler_params=params(limit=SMALL_LIMIT),
        cost_estimate=pl.CostEstimate(
            flops=2 * x.size * weight.shape[1], bytes_accessed=4 * x.size, transcendentals=0
        ),
        name="project",
    )(core.astype(jnp.int32).reshape(1), x, weight)


def gate_up_kernel(x_ref, perm_ref, gain_ref, gate_hbm, up_hbm, out_ref, gate_ref, up_ref, sem):
    experts, _, width = gate_ref.shape
    count = x_ref.shape[0] // experts
    copies = [
        [
            pltpu.make_async_copy(gate_hbm.at[e], gate_ref.at[e], sem.at[0, e]),
            pltpu.make_async_copy(up_hbm.at[e], up_ref.at[e], sem.at[1, e]),
        ]
        for e in range(experts)
    ]
    for pair in copies:
        for copy in pair:
            copy.start()
    for e in range(experts):
        at = slice(e * count, (e + 1) * count)
        rows = jnp.dot(perm_ref[at, :], x_ref[...], preferred_element_type=jnp.float32)
        scaled = (rows * gain_ref[...]).astype(jnp.bfloat16)
        squares = jnp.sum(rows * rows, axis=1, keepdims=True)
        high, mid, _ = split_bf16(squares)
        lane = lax.broadcasted_iota(jnp.int32, (count, LANES), 1)
        pad = jnp.where(lane == 0, high.astype(jnp.float32), 0.0)
        pad = jnp.where(lane == 1, mid.astype(jnp.float32), pad)
        out_ref[at, 2 * width :] = pad.astype(jnp.bfloat16)
        copies[e][0].wait()
        out_ref[at, :width] = jnp.dot(
            scaled, gate_ref[e], preferred_element_type=jnp.float32
        ).astype(jnp.bfloat16)
        copies[e][1].wait()
        out_ref[at, width : 2 * width] = jnp.dot(
            scaled, up_ref[e], preferred_element_type=jnp.float32
        ).astype(jnp.bfloat16)


def gate_up(x, perm, gain, gate_proj, up_proj):
    experts, depth, ff = gate_proj.shape
    slots = x.shape[0]
    vmem = pl.BlockSpec(memory_space=pltpu.VMEM)
    anywhere = pl.BlockSpec(memory_space=pl.ANY)
    return pl.pallas_call(
        gate_up_kernel,
        in_specs=[vmem] * 3 + [anywhere] * 2,
        out_specs=vmem,
        out_shape=jax.ShapeDtypeStruct((slots, 2 * ff + LANES), jnp.bfloat16),
        scratch_shapes=[
            pltpu.VMEM(gate_proj.shape, jnp.bfloat16),
            pltpu.VMEM(up_proj.shape, jnp.bfloat16),
            pltpu.SemaphoreType.DMA((2, experts)),
        ],
        compiler_params=params(limit=LARGE_LIMIT),
        cost_estimate=pl.CostEstimate(
            flops=4 * slots * depth * ff,
            bytes_accessed=4 * experts * depth * ff + 4 * slots * ff,
            transcendentals=0,
        ),
        name="gate_up",
    )(x, perm, gain, gate_proj, up_proj)


def activate_kernel(x_ref, out_ref):
    parts, rows, ff = out_ref.shape
    squares = jnp.zeros((rows, 1), jnp.float32)
    for part in range(parts):
        pad = x_ref[part, :, 2 * ff :].astype(jnp.float32)
        squares = squares + pad[:, 0:1] + pad[:, 1:2]
    inv_rms = lax.rsqrt(squares / D + EPSILON)
    step = 256
    for at in range(0, ff, step):
        gate = jnp.zeros((rows, step), jnp.float32)
        up = jnp.zeros((rows, step), jnp.float32)
        for part in range(parts):
            gate = gate + x_ref[part, :, at : at + step].astype(jnp.float32)
            up = up + x_ref[part, :, ff + at : ff + at + step].astype(jnp.float32)
        gate = gate * inv_rms
        up = up * inv_rms
        result = (gate / (1.0 + jnp.exp(-gate)) * up).astype(jnp.bfloat16)
        for part in range(parts):
            out_ref[part, :, at : at + step] = result


def activate(parts):
    count, rows, width = parts.shape
    return pl.pallas_call(
        activate_kernel,
        out_shape=jax.ShapeDtypeStruct((count, rows, (width - LANES) // 2), jnp.bfloat16),
        compiler_params=params(limit=SMALL_LIMIT),
        name="activate",
    )(parts)


def down_kernel(act_ref, back_ref, down_hbm, out_ref, all_ref, down_ref, sem):
    experts = down_ref.shape[0]
    count = act_ref.shape[0] // experts
    copies = [
        pltpu.make_async_copy(down_hbm.at[e], down_ref.at[e], sem.at[e]) for e in range(experts)
    ]
    for copy in copies:
        copy.start()
    for e in range(experts):
        at = slice(e * count, (e + 1) * count)
        copies[e].wait()
        all_ref[at, :] = jnp.dot(
            act_ref[at, :], down_ref[e], preferred_element_type=jnp.float32
        ).astype(jnp.bfloat16)
    out_ref[...] = jnp.dot(
        back_ref[...], all_ref[...], preferred_element_type=jnp.float32
    ).astype(jnp.bfloat16)


def down(act, back, down_proj):
    experts, ff, width = down_proj.shape
    slots = act.shape[0]
    vmem = pl.BlockSpec(memory_space=pltpu.VMEM)
    return pl.pallas_call(
        down_kernel,
        in_specs=[vmem] * 2 + [pl.BlockSpec(memory_space=pl.ANY)],
        out_specs=vmem,
        out_shape=jax.ShapeDtypeStruct((slots, width), jnp.bfloat16),
        scratch_shapes=[
            pltpu.VMEM((slots, width), jnp.bfloat16),
            pltpu.VMEM(down_proj.shape, jnp.bfloat16),
            pltpu.SemaphoreType.DMA((experts,)),
        ],
        compiler_params=params(limit=LARGE_LIMIT),
        cost_estimate=pl.CostEstimate(
            flops=2 * slots * ff * width,
            bytes_accessed=2 * experts * ff * width,
            transcendentals=0,
        ),
        name="down",
    )(act, back, down_proj)


def per_device(
    queries,
    tree_key_cache,
    tree_value_cache,
    tree_mask,
    lengths,
    out_weight,
    residual,
    norm_gain,
    expert_ids,
    gate_weights,
    gate_proj,
    up_proj,
    down_proj,
):
    rows = queries.shape[0]
    blocks, part_tokens = tree_key_cache.shape[:2]
    n_blk = lax.axis_size(BLK)
    n_narrow = lax.axis_size(NARROW)
    zl, x, core = (lax.axis_index(name) for name in BLK)
    zh, yh, yl = (lax.axis_index(name) for name in NARROW)
    kv_head = yh * 2 + yl
    heads = QUERY_HEADS // n_narrow
    width = heads * HEAD_SIZE
    swap = [(0, 1), (1, 0)]
    size_x = lax.axis_size("x")

    def head_piece(head):
        at = head * HEAD_SIZE
        return jnp.stack(
            [
                lax.dynamic_slice_in_dim(cache, at, HEAD_SIZE, 2)
                for cache in (tree_key_cache, tree_value_cache)
            ]
        )

    pieces = [head_piece(kv_head ^ step) for step in range(KEY_VALUE_HEADS)]
    kv = [pieces[0]]
    for step in (2, 1, 3):
        pairs = [(i, i ^ step) for i in range(KEY_VALUE_HEADS)]
        kv.append(lax.ppermute(pieces[step], ("yh", "yl"), pairs))
    kv = kv + [lax.ppermute(piece, "core", swap) for piece in kv]
    sources = [zh * KEY_VALUE_HEADS + (kv_head ^ s) for s in (0, 2, 1, 3)]

    both = lax.dynamic_slice_in_dim(queries, kv_head * 2 * width, 2 * width, 1)
    both = both.reshape(rows, 2, 2, width // 2)
    extra = jnp.concatenate(
        [
            tree_mask.astype(jnp.bfloat16),
            (lengths // 256).astype(jnp.bfloat16)[:, None],
            (lengths % 256).astype(jnp.bfloat16)[:, None],
            jnp.zeros((rows, LANES - TREE_BLOCKS - 2), jnp.bfloat16) + pieces[1][0, 0, 0, 0] * 0,
        ],
        axis=1,
    )
    own_q = lax.dynamic_index_in_dim(both, core, 2, False).reshape(rows, width)
    other_q = lax.dynamic_index_in_dim(both, 1 - core, 2, False).reshape(rows, width)
    own_q = jnp.concatenate([own_q, extra], axis=1)
    other_q = lax.ppermute(jnp.concatenate([other_q, extra], axis=1), "core", swap)
    pair = jnp.concatenate([own_q, other_q], axis=0)
    far = lax.ppermute(pair, "zl", swap)
    pair = jnp.concatenate([pair, far], axis=0)

    all_q, groups = [pair], []
    for dx in range(size_x):
        if dx:
            pairs = [(i, (i + dx) % size_x) for i in range(size_x)]
            all_q.append(lax.ppermute(pair, "x", pairs))
        for dz in range(2):
            origin = (zl ^ dz) * size_x + (x - dx) % size_x
            groups += [origin * 2 + core, origin * 2 + (1 - core)]
    zero = jnp.int32(0)
    info = [zl * size_x + x, core, zero, zero] + sources + groups
    info = jnp.stack([value.astype(jnp.int32) for value in info])
    group_axes = ("zl", "x", "zh")
    partial = attention(info, all_q, kv)
    partial = lax.all_to_all(partial.reshape(n_blk, rows, width + LANES), group_axes, 0, 0)
    attended = combine(partial, heads)

    gathered = jnp.zeros((KEY_VALUE_HEADS,) + attended.shape, attended.dtype)
    gathered = lax.dynamic_update_index_in_dim(gathered, attended, kv_head, 0)
    for step in range(1, KEY_VALUE_HEADS):
        pairs = [(i, i ^ step) for i in range(KEY_VALUE_HEADS)]
        piece = lax.ppermute(attended, ("yh", "yl"), pairs)
        gathered = lax.dynamic_update_index_in_dim(gathered, piece, kv_head ^ step, 0)
    gathered = gathered.reshape(n_blk // 2, 1, rows, -1)
    gathered = jnp.broadcast_to(gathered, (n_blk // 2, 2) + gathered.shape[2:])
    gathered = lax.all_to_all(gathered.reshape((n_blk,) + gathered.shape[2:]), group_axes, 0, 0)
    mine, other = project(core, gathered.reshape(n_blk // 2, 2, rows, -1), out_weight)
    projected = (mine + lax.ppermute(other, "core", swap).astype(jnp.float32)).astype(jnp.bfloat16)
    projected = projected.reshape(n_blk // 2, rows, -1)
    projected = lax.all_to_all(projected, ("zl", "x"), 0, 0)
    projected = jnp.sum(projected.astype(jnp.float32), axis=0)
    hidden_b = (residual.astype(jnp.float32) + projected).astype(jnp.bfloat16)

    exp_dev = gate_proj.shape[0]
    n_experts = exp_dev * n_blk
    flat_ids = expert_ids.reshape(-1)
    expert_hot = (flat_ids[:, None] == jnp.arange(n_experts)[None, :]).astype(jnp.int32)
    earlier = jnp.cumsum(expert_hot, axis=0) - expert_hot
    slot_of = jnp.sum(earlier * expert_hot, axis=1)
    target = (flat_ids * CAP + slot_of).reshape(rows, TOP)
    slots = n_experts * CAP
    at_slot = target[:, :, None] == jnp.arange(slots)[None, None, :]
    select = jnp.any(at_slot, axis=1).astype(jnp.bfloat16)
    mixing = jnp.sum(jnp.where(at_slot, gate_weights[:, :, None], 0.0), axis=1)
    outgoing = lax.dot_general(
        select, hidden_b, (((0,), (0,)), ((), ())), preferred_element_type=jnp.float32
    ).astype(jnp.bfloat16)
    incoming = lax.all_to_all(outgoing.reshape(n_blk, exp_dev * CAP, -1), BLK, 0, 0)

    place = jnp.arange(slots)
    expert, rest = place // (n_blk * CAP), place % (n_blk * CAP)
    order = (rest // CAP) * (exp_dev * CAP) + expert * CAP + rest % CAP
    perm = (order[:, None] == place[None, :]).astype(jnp.bfloat16)

    back = (place[:, None] == order[None, :]).astype(jnp.bfloat16)
    sums = gate_up(
        incoming.reshape(slots, -1), perm, norm_gain.reshape(1, -1), gate_proj, up_proj
    )
    sums = lax.all_to_all(sums.reshape(n_narrow, slots // n_narrow, -1), NARROW, 0, 0)
    activated = activate(sums)
    activated = lax.all_to_all(activated, NARROW, 0, 0).reshape(slots, -1)
    expert_out = down(activated, back, down_proj)
    returned = lax.all_to_all(expert_out.reshape(n_blk, exp_dev * CAP, -1), BLK, 0, 0)
    returned = returned.reshape(slots, -1)
    mix_high = lax.reduce_precision(mixing, 8, 7)
    mix_low = mixing - mix_high
    mixed_in = jnp.dot(
        mix_high.astype(jnp.bfloat16), returned, preferred_element_type=jnp.float32
    ) + jnp.dot(mix_low.astype(jnp.bfloat16), returned, preferred_element_type=jnp.float32)
    return (hidden_b.astype(jnp.float32) + mixed_in).astype(jnp.bfloat16)


def solution(mesh):
    shape = (2, 4, 2, 2, 2, 2)
    fine = Mesh(mesh.devices.reshape(shape), BLK + NARROW)
    in_specs = (
        P(BLK, None),
        P(BLK, NARROW, None),
        P(BLK, NARROW, None),
        P(BLK, None),
        P(BLK),
        P(BLK, NARROW),
        P(BLK, NARROW),
        P(NARROW),
        P(BLK, None),
        P(BLK, None),
        P(BLK, NARROW, None),
        P(BLK, NARROW, None),
        P(BLK, None, NARROW),
    )
    out_specs = P(BLK, NARROW)
    return jax.shard_map(
        per_device, mesh=fine, in_specs=in_specs, out_specs=out_specs, check_vma=False
    )
```

```python
import functools

import jax
import jax.numpy as jnp
from jax import lax
from jax.experimental import pallas as pl
from jax.experimental.pallas import tpu as pltpu
from jax.sharding import Mesh
from jax.sharding import PartitionSpec as P

D = 4096
QUERY_HEADS = 64
KEY_VALUE_HEADS = 4
HEAD_SIZE = 128
FF = 1536
TOP = 8
CAP = 6
BLOCK_TOKENS = 1024
TREE_BLOCKS = 64
NEGATIVE_FILLER = -1e30
EPSILON = 1e-06
SCORE_SCALE = HEAD_SIZE ** (-0.5)
LOG2E = 1.4426950408889634
LANES = 128
BLK = ("zl", "x", "core")
NARROW = ("zh", "yh", "yl")
SAFE_POWER = 100.0
VMEM_LIMIT = 40 * 1024 * 1024
LARGE_LIMIT = 56 * 1024 * 1024
SMALL_LIMIT = 12 * 1024 * 1024


def params(limit):
    return pltpu.CompilerParams(vmem_limit_bytes=limit)


def split_bf16(value):
    high = value.astype(jnp.bfloat16)
    rest = value - high.astype(jnp.float32)
    mid = rest.astype(jnp.bfloat16)
    low = (rest - mid.astype(jnp.float32)).astype(jnp.bfloat16)
    return high, mid, low


def attention_kernel(heads, info_ref, *refs):
    q_in = refs[0:4]
    kv_in = refs[4:12]
    out_ref, q_ref, k_ref, v_ref, vt_ref, lim_ref, mask_ref, s_ref, lse_ref, sem = refs[12:]
    rows = q_ref.shape[0]
    base = heads * HEAD_SIZE
    chip, core = info_ref[0], info_ref[1]
    chip_blocks, sources = k_ref.shape[:2]
    blocks = chip_blocks // 2
    span = sources * LANES
    tokens = chip_blocks * span
    step = rows // len(q_in)
    factor = SCORE_SCALE * LOG2E

    copies = []
    for i, ref in enumerate(q_in):
        at = pl.ds(i * step, step)
        copies.append(pltpu.make_async_copy(ref, q_ref.at[at], sem.at[len(copies)]))
    for i, ref in enumerate(kv_in):
        side, s = i // sources, i % sources
        for part, target in enumerate((k_ref, v_ref)):
            to = target.at[pl.ds(side * blocks, blocks), s]
            copies.append(pltpu.make_async_copy(ref.at[part], to, sem.at[len(copies)]))
    for copy in copies:
        copy.start()

    sub = lax.broadcasted_iota(jnp.int32, (16, tokens), 0)
    vt_ref[HEAD_SIZE:, :] = jnp.where(sub == 0, 1.0, 0.0).astype(jnp.bfloat16)
    for copy in copies[: len(q_in)]:
        copy.wait()
    extra = q_ref[:, base:].astype(jnp.float32).T
    lim_ref[...] = extra
    length = extra[TREE_BLOCKS : TREE_BLOCKS + 1] * 256.0 + extra[TREE_BLOCKS + 1 : TREE_BLOCKS + 2]
    first = pl.multiple_of(chip * chip_blocks, chip_blocks)
    reads = lim_ref[pl.ds(first, chip_blocks), :]
    block_id = lax.broadcasted_iota(jnp.int32, (chip_blocks, rows), 0) + first
    bound = length - (block_id * BLOCK_TOKENS).astype(jnp.float32)
    lim_ref[0:chip_blocks, :] = jnp.where(reads > 0.5, bound, 0.0)
    most_q = jnp.zeros((rows, 1), jnp.float32)
    for h in range(heads):
        q = q_ref[:, h * HEAD_SIZE : (h + 1) * HEAD_SIZE].astype(jnp.float32)
        most_q = jnp.maximum(most_q, jnp.sum(q * q, axis=1, keepdims=True))
    token = lax.broadcasted_iota(jnp.int32, (LANES, 1), 0)
    token = [(token + info_ref[4 + s] * LANES).astype(jnp.float32) for s in range(sources)]
    token = jnp.concatenate(token, axis=0)
    for i in range(chip_blocks):
        at = slice(i * span, (i + 1) * span)
        side = core if i < blocks else 1 - core
        lim = lim_ref[pl.ds(side * blocks + i % blocks, 1), :]
        mask_ref[at, :] = jnp.where(token < lim, 1.0, 0.0).astype(jnp.bfloat16)
    for copy in copies[len(q_in) :]:
        copy.wait()
    most_k = jnp.zeros((LANES, HEAD_SIZE), jnp.float32)
    for i in range(chip_blocks):
        vt_ref[:HEAD_SIZE, i * span : (i + 1) * span] = v_ref[i].reshape(span, HEAD_SIZE).T
        for s in range(sources):
            keys = k_ref[i, s].astype(jnp.float32)
            most_k = jnp.maximum(most_k, keys * keys)
    most_k = jnp.sum(jnp.max(most_k, axis=0, keepdims=True), axis=1, keepdims=True)
    most = jnp.max(most_q) * jnp.max(most_k) * (factor * factor)
    small = most <= SAFE_POWER * SAFE_POWER

    def finish(h, cols, acc, top):
        total = acc[HEAD_SIZE : HEAD_SIZE + 1]
        some = total > 0
        safe = jnp.where(some, total, 1.0)
        result = (acc[:HEAD_SIZE] / safe).astype(jnp.bfloat16).T
        group = rows // 16
        for i in range(16):
            row = pl.multiple_of(info_ref[8 + i] * group, group)
            out_ref[pl.ds(row, group), cols] = result[i * group : (i + 1) * group]
        lse = jnp.where(some, top * SCORE_SCALE + jnp.log(safe), NEGATIVE_FILLER)
        lse_ref[pl.ds(h, 1), :] = lse

    def head_columns(h):
        return pl.ds(pl.multiple_of(h * HEAD_SIZE, HEAD_SIZE), HEAD_SIZE)

    chunk = 2

    def small_head(h, carry):
        cols = head_columns(h)
        qt = q_ref[:, cols].T
        acc = jnp.zeros((HEAD_SIZE + 16, rows), jnp.float32)
        for i in range(0, chip_blocks, chunk):
            at = slice(i * span, (i + chunk) * span)
            keys = k_ref[i : i + chunk].reshape(chunk * span, HEAD_SIZE)
            s = jnp.dot(keys, qt, preferred_element_type=jnp.float32) * factor
            p = jnp.exp2(s).astype(jnp.bfloat16) * mask_ref[at, :]
            acc = acc + jnp.dot(vt_ref[:, at], p, preferred_element_type=jnp.float32)
        finish(h, cols, acc, 0.0)
        return carry

    def any_head(h, carry):
        cols = head_columns(h)
        qt = q_ref[:, cols].T
        top = jnp.full((1, rows), -1e29, jnp.float32)
        for i in range(chip_blocks):
            at = slice(i * span, (i + 1) * span)
            keys = k_ref[i].reshape(span, HEAD_SIZE)
            s = jnp.dot(keys, qt, preferred_element_type=jnp.float32)
            s = jnp.where(mask_ref[at, :].astype(jnp.float32) > 0.5, s, NEGATIVE_FILLER)
            s_ref[at, :] = s
            top = jnp.maximum(top, jnp.max(s, axis=0, keepdims=True))
        acc = jnp.zeros((HEAD_SIZE + 16, rows), jnp.float32)
        for i in range(chip_blocks):
            at = slice(i * span, (i + 1) * span)
            p = jnp.exp2((s_ref[at, :] - top) * factor).astype(jnp.bfloat16)
            acc = acc + jnp.dot(vt_ref[:, at], p, preferred_element_type=jnp.float32)
        finish(h, cols, acc, top)
        return carry

    @pl.when(small)
    def _():
        lax.fori_loop(0, heads, small_head, 0, unroll=2)

    @pl.when(jnp.logical_not(small))
    def _():
        lax.fori_loop(0, heads, any_head, 0)

    high, mid, low = split_bf16(lse_ref[...])
    pieces = [piece.astype(jnp.float32) for piece in (high, mid, low)]
    pieces.append(jnp.zeros((LANES - 3 * heads, rows), jnp.float32))
    result = jnp.concatenate(pieces, axis=0).T.astype(jnp.bfloat16)
    group = rows // 16
    for i in range(16):
        row = pl.multiple_of(info_ref[8 + i] * group, group)
        out_ref[pl.ds(row, group), base:] = result[i * group : (i + 1) * group]


def attention(info, queries, kv):
    step, width = queries[0].shape
    rows = step * len(queries)
    heads = (width - LANES) // HEAD_SIZE
    blocks = kv[0].shape[1]
    sources = len(kv) // 2
    tokens = len(kv) * blocks * LANES
    anywhere = pl.BlockSpec(memory_space=pl.ANY)
    tiles = (2 * blocks, sources, LANES, HEAD_SIZE)
    return pl.pallas_call(
        functools.partial(attention_kernel, heads),
        in_specs=[pl.BlockSpec(memory_space=pltpu.SMEM)] + [anywhere] * (len(queries) + len(kv)),
        out_specs=pl.BlockSpec(memory_space=pltpu.VMEM),
        out_shape=jax.ShapeDtypeStruct((rows, width), jnp.bfloat16),
        scratch_shapes=[
            pltpu.VMEM((rows, width), jnp.bfloat16),
            pltpu.VMEM(tiles, jnp.bfloat16),
            pltpu.VMEM(tiles, jnp.bfloat16),
            pltpu.VMEM((HEAD_SIZE + 16, tokens), jnp.bfloat16),
            pltpu.VMEM((LANES, rows), jnp.float32),
            pltpu.VMEM((tokens, rows), jnp.bfloat16),
            pltpu.VMEM((tokens, rows), jnp.float32),
            pltpu.VMEM((heads, rows), jnp.float32),
            pltpu.SemaphoreType.DMA((len(queries) + 2 * len(kv),)),
        ],
        compiler_params=params(limit=VMEM_LIMIT),
        cost_estimate=pl.CostEstimate(
            flops=6 * rows * heads * tokens * HEAD_SIZE,
            bytes_accessed=6 << 20,
            transcendentals=rows * heads * tokens,
        ),
        name="attention",
    )(info, *queries, *kv)


def combine_kernel(heads, x_ref, out_ref):
    base = heads * HEAD_SIZE
    info = x_ref[:, :, base:].astype(jnp.float32)
    for h in range(heads):
        lse = info[:, :, h : h + 1] + info[:, :, 8 + h : 9 + h]
        lse = lse + info[:, :, 16 + h : 17 + h]
        scale = jnp.exp(lse - jnp.max(lse, axis=0, keepdims=True))
        cols = slice(h * HEAD_SIZE, (h + 1) * HEAD_SIZE)
        acc = jnp.sum(x_ref[:, :, cols].astype(jnp.float32) * scale, axis=0)
        at = h % (heads // 2) * HEAD_SIZE
        out_ref[h // (heads // 2), :, at : at + HEAD_SIZE] = (
            acc / jnp.sum(scale, axis=0)
        ).astype(jnp.bfloat16)


def combine(parts, heads):
    _, rows, _ = parts.shape
    return pl.pallas_call(
        functools.partial(combine_kernel, heads),
        out_shape=jax.ShapeDtypeStruct((2, rows, heads * HEAD_SIZE // 2), jnp.bfloat16),
        compiler_params=params(limit=SMALL_LIMIT),
        cost_estimate=pl.CostEstimate(
            flops=4 * parts.size, bytes_accessed=2 * parts.size, transcendentals=0
        ),
        name="combine",
    )(parts)


def project_kernel(core_ref, x_ref, weight_ref, mine_ref, other_ref):
    chips, _, rows, depth = x_ref.shape
    core = core_ref[0]
    for ref, side in ((other_ref, 1 - core), (mine_ref, core)):
        x = x_ref[:, pl.ds(side, 1)].reshape(chips * rows, depth)
        product = jnp.dot(x, weight_ref[...], preferred_element_type=jnp.float32)
        ref[...] = product.astype(ref.dtype)


def project(core, x, weight):
    chips, _, rows, _ = x.shape
    shape = (chips * rows, weight.shape[1])
    vmem = pl.BlockSpec(memory_space=pltpu.VMEM)
    return pl.pallas_call(
        project_kernel,
        in_specs=[pl.BlockSpec(memory_space=pltpu.SMEM), vmem, vmem],
        out_specs=[vmem, vmem],
        out_shape=[
            jax.ShapeDtypeStruct(shape, jnp.float32),
            jax.ShapeDtypeStruct(shape, jnp.bfloat16),
        ],
        compiler_params=params(limit=SMALL_LIMIT),
        cost_estimate=pl.CostEstimate(
            flops=2 * x.size * weight.shape[1], bytes_accessed=4 * x.size, transcendentals=0
        ),
        name="project",
    )(core.astype(jnp.int32).reshape(1), x, weight)


def gate_up_kernel(x_ref, perm_ref, gain_ref, gate_hbm, up_hbm, out_ref, gate_ref, up_ref, sem):
    experts, _, width = gate_ref.shape
    count = x_ref.shape[0] // experts
    copies = [
        [
            pltpu.make_async_copy(gate_hbm.at[e], gate_ref.at[e], sem.at[0, e]),
            pltpu.make_async_copy(up_hbm.at[e], up_ref.at[e], sem.at[1, e]),
        ]
        for e in range(experts)
    ]
    for pair in copies:
        for copy in pair:
            copy.start()
    for e in range(experts):
        at = slice(e * count, (e + 1) * count)
        rows = jnp.dot(perm_ref[at, :], x_ref[...], preferred_element_type=jnp.float32)
        scaled = (rows * gain_ref[0:1, :]).astype(jnp.bfloat16)
        squares = jnp.sum(rows * rows, axis=1, keepdims=True)
        high, mid, _ = split_bf16(squares)
        lane = lax.broadcasted_iota(jnp.int32, (count, LANES), 1)
        pad = jnp.where(lane == 0, high.astype(jnp.float32), 0.0)
        pad = jnp.where(lane == 1, mid.astype(jnp.float32), pad)
        out_ref[at, 2 * width :] = pad.astype(jnp.bfloat16)
        copies[e][0].wait()
        out_ref[at, :width] = jnp.dot(
            scaled, gate_ref[e], preferred_element_type=jnp.float32
        ).astype(jnp.bfloat16)
        copies[e][1].wait()
        out_ref[at, width : 2 * width] = jnp.dot(
            scaled, up_ref[e], preferred_element_type=jnp.float32
        ).astype(jnp.bfloat16)


def gate_up(x, perm, gain, gate_proj, up_proj):
    experts, depth, ff = gate_proj.shape
    slots = x.shape[0]
    vmem = pl.BlockSpec(memory_space=pltpu.VMEM)
    anywhere = pl.BlockSpec(memory_space=pl.ANY)
    return pl.pallas_call(
        gate_up_kernel,
        in_specs=[vmem] * 3 + [anywhere] * 2,
        out_specs=vmem,
        out_shape=jax.ShapeDtypeStruct((slots, 2 * ff + LANES), jnp.bfloat16),
        scratch_shapes=[
            pltpu.VMEM(gate_proj.shape, jnp.bfloat16),
            pltpu.VMEM(up_proj.shape, jnp.bfloat16),
            pltpu.SemaphoreType.DMA((2, experts)),
        ],
        compiler_params=params(limit=LARGE_LIMIT),
        cost_estimate=pl.CostEstimate(
            flops=4 * slots * depth * ff,
            bytes_accessed=4 * experts * depth * ff + 4 * slots * ff,
            transcendentals=0,
        ),
        name="gate_up",
    )(x, perm, gain, gate_proj, up_proj)


def activate_kernel(x_ref, out_ref):
    parts, rows, ff = out_ref.shape
    squares = jnp.zeros((rows, 1), jnp.float32)
    for part in range(parts):
        pad = x_ref[part, :, 2 * ff :].astype(jnp.float32)
        squares = squares + pad[:, 0:1] + pad[:, 1:2]
    inv_rms = lax.rsqrt(squares / D + EPSILON)
    step = 256
    for at in range(0, ff, step):
        gate = jnp.zeros((rows, step), jnp.float32)
        up = jnp.zeros((rows, step), jnp.float32)
        for part in range(parts):
            gate = gate + x_ref[part, :, at : at + step].astype(jnp.float32)
            up = up + x_ref[part, :, ff + at : ff + at + step].astype(jnp.float32)
        gate = gate * inv_rms
        up = up * inv_rms
        result = (gate / (1.0 + jnp.exp(-gate)) * up).astype(jnp.bfloat16)
        for part in range(parts):
            out_ref[part, :, at : at + step] = result


def activate(parts):
    count, rows, width = parts.shape
    return pl.pallas_call(
        activate_kernel,
        out_shape=jax.ShapeDtypeStruct((count, rows, (width - LANES) // 2), jnp.bfloat16),
        compiler_params=params(limit=SMALL_LIMIT),
        name="activate",
    )(parts)


def down_kernel(act_ref, back_ref, down_hbm, out_ref, all_ref, down_ref, sem):
    experts = down_ref.shape[0]
    count = act_ref.shape[0] // experts
    copies = [
        pltpu.make_async_copy(down_hbm.at[e], down_ref.at[e], sem.at[e]) for e in range(experts)
    ]
    for copy in copies:
        copy.start()
    for e in range(experts):
        at = slice(e * count, (e + 1) * count)
        copies[e].wait()
        all_ref[at, :] = jnp.dot(
            act_ref[at, :], down_ref[e], preferred_element_type=jnp.float32
        ).astype(jnp.bfloat16)
    out_ref[...] = jnp.dot(
        back_ref[...], all_ref[...], preferred_element_type=jnp.float32
    ).astype(jnp.bfloat16)


def down(act, back, down_proj):
    experts, ff, width = down_proj.shape
    slots = act.shape[0]
    vmem = pl.BlockSpec(memory_space=pltpu.VMEM)
    return pl.pallas_call(
        down_kernel,
        in_specs=[vmem] * 2 + [pl.BlockSpec(memory_space=pl.ANY)],
        out_specs=vmem,
        out_shape=jax.ShapeDtypeStruct((slots, width), jnp.bfloat16),
        scratch_shapes=[
            pltpu.VMEM((slots, width), jnp.bfloat16),
            pltpu.VMEM(down_proj.shape, jnp.bfloat16),
            pltpu.SemaphoreType.DMA((experts,)),
        ],
        compiler_params=params(limit=LARGE_LIMIT),
        cost_estimate=pl.CostEstimate(
            flops=2 * slots * ff * width,
            bytes_accessed=2 * experts * ff * width,
            transcendentals=0,
        ),
        name="down",
    )(act, back, down_proj)


def per_device(
    queries,
    tree_key_cache,
    tree_value_cache,
    tree_mask,
    lengths,
    out_weight,
    residual,
    norm_gain,
    expert_ids,
    gate_weights,
    gate_proj,
    up_proj,
    down_proj,
):
    rows = queries.shape[0]
    blocks, part_tokens = tree_key_cache.shape[:2]
    n_blk = lax.axis_size(BLK)
    n_narrow = lax.axis_size(NARROW)
    zl, x, core = (lax.axis_index(name) for name in BLK)
    zh, yh, yl = (lax.axis_index(name) for name in NARROW)
    kv_head = yh * 2 + yl
    heads = QUERY_HEADS // n_narrow
    width = heads * HEAD_SIZE
    swap = [(0, 1), (1, 0)]
    size_x = lax.axis_size("x")

    def head_piece(head):
        at = head * HEAD_SIZE
        return jnp.stack(
            [
                lax.dynamic_slice_in_dim(cache, at, HEAD_SIZE, 2)
                for cache in (tree_key_cache, tree_value_cache)
            ]
        )

    pieces = [head_piece(kv_head ^ step) for step in range(KEY_VALUE_HEADS)]
    kv = [pieces[0]]
    for step in (2, 1, 3):
        pairs = [(i, i ^ step) for i in range(KEY_VALUE_HEADS)]
        kv.append(lax.ppermute(pieces[step], ("yh", "yl"), pairs))
    kv = kv + [lax.ppermute(piece, "core", swap) for piece in kv]
    sources = [zh * KEY_VALUE_HEADS + (kv_head ^ s) for s in (0, 2, 1, 3)]

    both = lax.dynamic_slice_in_dim(queries, kv_head * 2 * width, 2 * width, 1)
    both = both.reshape(rows, 2, 2, width // 2)
    extra = jnp.concatenate(
        [
            tree_mask.astype(jnp.bfloat16),
            (lengths // 256).astype(jnp.bfloat16)[:, None],
            (lengths % 256).astype(jnp.bfloat16)[:, None],
            jnp.zeros((rows, LANES - TREE_BLOCKS - 2), jnp.bfloat16) + pieces[1][0, 0, 0, 0] * 0,
        ],
        axis=1,
    )
    own_q = lax.dynamic_index_in_dim(both, core, 2, False).reshape(rows, width)
    other_q = lax.dynamic_index_in_dim(both, 1 - core, 2, False).reshape(rows, width)
    own_q = jnp.concatenate([own_q, extra], axis=1)
    other_q = lax.ppermute(jnp.concatenate([other_q, extra], axis=1), "core", swap)
    pair = jnp.concatenate([own_q, other_q], axis=0)
    far = lax.ppermute(pair, "zl", swap)
    pair = jnp.concatenate([pair, far], axis=0)

    all_q, groups = [pair], []
    for dx in range(size_x):
        if dx:
            pairs = [(i, (i + dx) % size_x) for i in range(size_x)]
            all_q.append(lax.ppermute(pair, "x", pairs))
        for dz in range(2):
            origin = (zl ^ dz) * size_x + (x - dx) % size_x
            groups += [origin * 2 + core, origin * 2 + (1 - core)]
    zero = jnp.int32(0)
    info = [zl * size_x + x, core, zero, zero] + sources + groups
    info = jnp.stack([value.astype(jnp.int32) for value in info])
    group_axes = ("zl", "x", "zh")
    partial = attention(info, all_q, kv)
    partial = lax.all_to_all(partial.reshape(n_blk, rows, width + LANES), group_axes, 0, 0)
    attended = combine(partial, heads)

    gathered = jnp.zeros((KEY_VALUE_HEADS,) + attended.shape, attended.dtype)
    gathered = lax.dynamic_update_index_in_dim(gathered, attended, kv_head, 0)
    for step in range(1, KEY_VALUE_HEADS):
        pairs = [(i, i ^ step) for i in range(KEY_VALUE_HEADS)]
        piece = lax.ppermute(attended, ("yh", "yl"), pairs)
        gathered = lax.dynamic_update_index_in_dim(gathered, piece, kv_head ^ step, 0)
    gathered = gathered.reshape(n_blk // 2, 1, rows, -1)
    gathered = jnp.broadcast_to(gathered, (n_blk // 2, 2) + gathered.shape[2:])
    gathered = lax.all_to_all(gathered.reshape((n_blk,) + gathered.shape[2:]), group_axes, 0, 0)
    mine, other = project(core, gathered.reshape(n_blk // 2, 2, rows, -1), out_weight)
    projected = (mine + lax.ppermute(other, "core", swap).astype(jnp.float32)).astype(jnp.bfloat16)
    projected = projected.reshape(n_blk // 2, rows, -1)
    projected = lax.all_to_all(projected, ("zl", "x"), 0, 0)
    projected = jnp.sum(projected.astype(jnp.float32), axis=0)
    hidden_b = (residual.astype(jnp.float32) + projected).astype(jnp.bfloat16)

    exp_dev = gate_proj.shape[0]
    n_experts = exp_dev * n_blk
    flat_ids = expert_ids.reshape(-1)
    expert_hot = (flat_ids[:, None] == jnp.arange(n_experts)[None, :]).astype(jnp.int32)
    earlier = jnp.cumsum(expert_hot, axis=0) - expert_hot
    slot_of = jnp.sum(earlier * expert_hot, axis=1)
    target = (flat_ids * CAP + slot_of).reshape(rows, TOP)
    slots = n_experts * CAP
    at_slot = target[:, :, None] == jnp.arange(slots)[None, None, :]
    select = jnp.any(at_slot, axis=1).astype(jnp.bfloat16)
    mixing = jnp.sum(jnp.where(at_slot, gate_weights[:, :, None], 0.0), axis=1)
    outgoing = lax.dot_general(
        select, hidden_b, (((0,), (0,)), ((), ())), preferred_element_type=jnp.float32
    ).astype(jnp.bfloat16)
    incoming = lax.all_to_all(outgoing.reshape(n_blk, exp_dev * CAP, -1), BLK, 0, 0)

    place = jnp.arange(slots)
    expert, rest = place // (n_blk * CAP), place % (n_blk * CAP)
    order = (rest // CAP) * (exp_dev * CAP) + expert * CAP + rest % CAP
    perm = (order[:, None] == place[None, :]).astype(jnp.bfloat16)

    back = (place[:, None] == order[None, :]).astype(jnp.bfloat16)
    gain = jnp.broadcast_to(norm_gain[None], (8, norm_gain.shape[0])) + perm[0, 1] * 0
    sums = gate_up(
        incoming.reshape(slots, -1), perm, gain, gate_proj, up_proj
    )
    sums = lax.all_to_all(sums.reshape(n_narrow, slots // n_narrow, -1), NARROW, 0, 0)
    activated = activate(sums)
    activated = lax.all_to_all(activated, NARROW, 0, 0).reshape(slots, -1)
    expert_out = down(activated, back, down_proj)
    returned = lax.all_to_all(expert_out.reshape(n_blk, exp_dev * CAP, -1), BLK, 0, 0)
    returned = returned.reshape(slots, -1)
    mix_high = lax.reduce_precision(mixing, 8, 7)
    mix_low = mixing - mix_high
    mixed_in = jnp.dot(
        mix_high.astype(jnp.bfloat16), returned, preferred_element_type=jnp.float32
    ) + jnp.dot(mix_low.astype(jnp.bfloat16), returned, preferred_element_type=jnp.float32)
    return (hidden_b.astype(jnp.float32) + mixed_in).astype(jnp.bfloat16)


def solution(mesh):
    shape = (2, 4, 2, 2, 2, 2)
    fine = Mesh(mesh.devices.reshape(shape), BLK + NARROW)
    in_specs = (
        P(BLK, None),
        P(BLK, NARROW, None),
        P(BLK, NARROW, None),
        P(BLK, None),
        P(BLK),
        P(BLK, NARROW),
        P(BLK, NARROW),
        P(NARROW),
        P(BLK, None),
        P(BLK, None),
        P(BLK, NARROW, None),
        P(BLK, NARROW, None),
        P(BLK, None, NARROW),
    )
    out_specs = P(BLK, NARROW)
    return jax.shard_map(
        per_device, mesh=fine, in_specs=in_specs, out_specs=out_specs, check_vma=False
    )
```

```python
import functools

import jax
import jax.numpy as jnp
from jax import lax
from jax.experimental import pallas as pl
from jax.experimental.pallas import tpu as pltpu
from jax.sharding import Mesh
from jax.sharding import PartitionSpec as P

D = 4096
QUERY_HEADS = 64
KEY_VALUE_HEADS = 4
HEAD_SIZE = 128
FF = 1536
TOP = 8
CAP = 6
BLOCK_TOKENS = 1024
TREE_BLOCKS = 64
NEGATIVE_FILLER = -1e30
EPSILON = 1e-06
SCORE_SCALE = HEAD_SIZE ** (-0.5)
LOG2E = 1.4426950408889634
LANES = 128
BLK = ("zl", "x", "core")
NARROW = ("zh", "yh", "yl")
SAFE_POWER = 100.0
VMEM_LIMIT = 40 * 1024 * 1024
LARGE_LIMIT = 56 * 1024 * 1024
SMALL_LIMIT = 12 * 1024 * 1024


def params(limit):
    return pltpu.CompilerParams(vmem_limit_bytes=limit)


def split_bf16(value):
    high = value.astype(jnp.bfloat16)
    rest = value - high.astype(jnp.float32)
    mid = rest.astype(jnp.bfloat16)
    low = (rest - mid.astype(jnp.float32)).astype(jnp.bfloat16)
    return high, mid, low


def attention_kernel(heads, info_ref, *refs):
    q_in = refs[0:4]
    kv_in = refs[4:12]
    out_ref, q_ref, k_ref, v_ref, vt_ref, lim_ref, mask_ref, s_ref, lse_ref, sem = refs[12:]
    rows = q_ref.shape[0]
    base = heads * HEAD_SIZE
    chip, core = info_ref[0], info_ref[1]
    chip_blocks, sources = k_ref.shape[:2]
    blocks = chip_blocks // 2
    span = sources * LANES
    tokens = chip_blocks * span
    step = rows // len(q_in)
    factor = SCORE_SCALE * LOG2E

    copies = []
    for i, ref in enumerate(q_in):
        at = pl.ds(i * step, step)
        copies.append(pltpu.make_async_copy(ref, q_ref.at[at], sem.at[len(copies)]))
    for i, ref in enumerate(kv_in):
        side, s = i // sources, i % sources
        for part, target in enumerate((k_ref, v_ref)):
            to = target.at[pl.ds(side * blocks, blocks), s]
            copies.append(pltpu.make_async_copy(ref.at[part], to, sem.at[len(copies)]))
    for copy in copies:
        copy.start()

    sub = lax.broadcasted_iota(jnp.int32, (16, tokens), 0)
    vt_ref[HEAD_SIZE:, :] = jnp.where(sub == 0, 1.0, 0.0).astype(jnp.bfloat16)
    for copy in copies[: len(q_in)]:
        copy.wait()
    extra = q_ref[:, base:].astype(jnp.float32).T
    lim_ref[...] = extra
    length = extra[TREE_BLOCKS : TREE_BLOCKS + 1] * 256.0 + extra[TREE_BLOCKS + 1 : TREE_BLOCKS + 2]
    first = pl.multiple_of(chip * chip_blocks, chip_blocks)
    reads = lim_ref[pl.ds(first, chip_blocks), :]
    block_id = lax.broadcasted_iota(jnp.int32, (chip_blocks, rows), 0) + first
    bound = length - (block_id * BLOCK_TOKENS).astype(jnp.float32)
    lim_ref[0:chip_blocks, :] = jnp.where(reads > 0.5, bound, 0.0)
    most_q = jnp.zeros((rows, 1), jnp.float32)
    for h in range(heads):
        q = q_ref[:, h * HEAD_SIZE : (h + 1) * HEAD_SIZE].astype(jnp.float32)
        most_q = jnp.maximum(most_q, jnp.sum(q * q, axis=1, keepdims=True))
    token = lax.broadcasted_iota(jnp.int32, (LANES, 1), 0)
    token = [(token + info_ref[4 + s] * LANES).astype(jnp.float32) for s in range(sources)]
    token = jnp.concatenate(token, axis=0)
    for i in range(chip_blocks):
        at = slice(i * span, (i + 1) * span)
        side = core if i < blocks else 1 - core
        lim = lim_ref[pl.ds(side * blocks + i % blocks, 1), :]
        mask_ref[at, :] = jnp.where(token < lim, 1.0, 0.0).astype(jnp.bfloat16)
    for copy in copies[len(q_in) :]:
        copy.wait()
    most_k = jnp.zeros((LANES, HEAD_SIZE), jnp.float32)
    for i in range(chip_blocks):
        vt_ref[:HEAD_SIZE, i * span : (i + 1) * span] = v_ref[i].reshape(span, HEAD_SIZE).T
        for s in range(sources):
            keys = k_ref[i, s].astype(jnp.float32)
            most_k = jnp.maximum(most_k, keys * keys)
    most_k = jnp.sum(jnp.max(most_k, axis=0, keepdims=True), axis=1, keepdims=True)
    most = jnp.max(most_q) * jnp.max(most_k) * (factor * factor)
    small = most <= SAFE_POWER * SAFE_POWER

    def finish(h, cols, acc, top):
        total = acc[HEAD_SIZE : HEAD_SIZE + 1]
        some = total > 0
        safe = jnp.where(some, total, 1.0)
        result = (acc[:HEAD_SIZE] / safe).astype(jnp.bfloat16).T
        group = rows // 16
        for i in range(16):
            row = pl.multiple_of(info_ref[8 + i] * group, group)
            out_ref[pl.ds(row, group), cols] = result[i * group : (i + 1) * group]
        lse = jnp.where(some, top * SCORE_SCALE + jnp.log(safe), NEGATIVE_FILLER)
        lse_ref[pl.ds(h, 1), :] = lse

    def head_columns(h):
        return pl.ds(pl.multiple_of(h * HEAD_SIZE, HEAD_SIZE), HEAD_SIZE)

    chunk = 4

    def small_head(h, carry):
        cols = head_columns(h)
        qt = q_ref[:, cols].T
        acc = jnp.zeros((HEAD_SIZE + 16, rows), jnp.float32)
        for i in range(0, chip_blocks, chunk):
            at = slice(i * span, (i + chunk) * span)
            keys = k_ref[i : i + chunk].reshape(chunk * span, HEAD_SIZE)
            s = jnp.dot(keys, qt, preferred_element_type=jnp.float32) * factor
            p = jnp.exp2(s).astype(jnp.bfloat16) * mask_ref[at, :]
            acc = acc + jnp.dot(vt_ref[:, at], p, preferred_element_type=jnp.float32)
        finish(h, cols, acc, 0.0)
        return carry

    def any_head(h, carry):
        cols = head_columns(h)
        qt = q_ref[:, cols].T
        top = jnp.full((1, rows), -1e29, jnp.float32)
        for i in range(chip_blocks):
            at = slice(i * span, (i + 1) * span)
            keys = k_ref[i].reshape(span, HEAD_SIZE)
            s = jnp.dot(keys, qt, preferred_element_type=jnp.float32)
            s = jnp.where(mask_ref[at, :].astype(jnp.float32) > 0.5, s, NEGATIVE_FILLER)
            s_ref[at, :] = s
            top = jnp.maximum(top, jnp.max(s, axis=0, keepdims=True))
        acc = jnp.zeros((HEAD_SIZE + 16, rows), jnp.float32)
        for i in range(chip_blocks):
            at = slice(i * span, (i + 1) * span)
            p = jnp.exp2((s_ref[at, :] - top) * factor).astype(jnp.bfloat16)
            acc = acc + jnp.dot(vt_ref[:, at], p, preferred_element_type=jnp.float32)
        finish(h, cols, acc, top)
        return carry

    @pl.when(small)
    def _():
        lax.fori_loop(0, heads, small_head, 0, unroll=2)

    @pl.when(jnp.logical_not(small))
    def _():
        lax.fori_loop(0, heads, any_head, 0)

    high, mid, low = split_bf16(lse_ref[...])
    pieces = [piece.astype(jnp.float32) for piece in (high, mid, low)]
    pieces.append(jnp.zeros((LANES - 3 * heads, rows), jnp.float32))
    result = jnp.concatenate(pieces, axis=0).T.astype(jnp.bfloat16)
    group = rows // 16
    for i in range(16):
        row = pl.multiple_of(info_ref[8 + i] * group, group)
        out_ref[pl.ds(row, group), base:] = result[i * group : (i + 1) * group]


def attention(info, queries, kv):
    step, width = queries[0].shape
    rows = step * len(queries)
    heads = (width - LANES) // HEAD_SIZE
    blocks = kv[0].shape[1]
    sources = len(kv) // 2
    tokens = len(kv) * blocks * LANES
    anywhere = pl.BlockSpec(memory_space=pl.ANY)
    tiles = (2 * blocks, sources, LANES, HEAD_SIZE)
    return pl.pallas_call(
        functools.partial(attention_kernel, heads),
        in_specs=[pl.BlockSpec(memory_space=pltpu.SMEM)] + [anywhere] * (len(queries) + len(kv)),
        out_specs=pl.BlockSpec(memory_space=pltpu.VMEM),
        out_shape=jax.ShapeDtypeStruct((rows, width), jnp.bfloat16),
        scratch_shapes=[
            pltpu.VMEM((rows, width), jnp.bfloat16),
            pltpu.VMEM(tiles, jnp.bfloat16),
            pltpu.VMEM(tiles, jnp.bfloat16),
            pltpu.VMEM((HEAD_SIZE + 16, tokens), jnp.bfloat16),
            pltpu.VMEM((LANES, rows), jnp.float32),
            pltpu.VMEM((tokens, rows), jnp.bfloat16),
            pltpu.VMEM((tokens, rows), jnp.float32),
            pltpu.VMEM((heads, rows), jnp.float32),
            pltpu.SemaphoreType.DMA((len(queries) + 2 * len(kv),)),
        ],
        compiler_params=params(limit=VMEM_LIMIT),
        cost_estimate=pl.CostEstimate(
            flops=6 * rows * heads * tokens * HEAD_SIZE,
            bytes_accessed=6 << 20,
            transcendentals=rows * heads * tokens,
        ),
        name="attention",
    )(info, *queries, *kv)


def combine_kernel(heads, x_ref, out_ref):
    base = heads * HEAD_SIZE
    info = x_ref[:, :, base:].astype(jnp.float32)
    for h in range(heads):
        lse = info[:, :, h : h + 1] + info[:, :, 8 + h : 9 + h]
        lse = lse + info[:, :, 16 + h : 17 + h]
        scale = jnp.exp(lse - jnp.max(lse, axis=0, keepdims=True))
        cols = slice(h * HEAD_SIZE, (h + 1) * HEAD_SIZE)
        acc = jnp.sum(x_ref[:, :, cols].astype(jnp.float32) * scale, axis=0)
        at = h % (heads // 2) * HEAD_SIZE
        out_ref[h // (heads // 2), :, at : at + HEAD_SIZE] = (
            acc / jnp.sum(scale, axis=0)
        ).astype(jnp.bfloat16)


def combine(parts, heads):
    _, rows, _ = parts.shape
    return pl.pallas_call(
        functools.partial(combine_kernel, heads),
        out_shape=jax.ShapeDtypeStruct((2, rows, heads * HEAD_SIZE // 2), jnp.bfloat16),
        compiler_params=params(limit=SMALL_LIMIT),
        cost_estimate=pl.CostEstimate(
            flops=4 * parts.size, bytes_accessed=2 * parts.size, transcendentals=0
        ),
        name="combine",
    )(parts)


def project_kernel(core_ref, x_ref, weight_ref, mine_ref, other_ref):
    chips, _, rows, depth = x_ref.shape
    core = core_ref[0]
    for ref, side in ((other_ref, 1 - core), (mine_ref, core)):
        x = x_ref[:, pl.ds(side, 1)].reshape(chips * rows, depth)
        product = jnp.dot(x, weight_ref[...], preferred_element_type=jnp.float32)
        ref[...] = product.astype(ref.dtype)


def project(core, x, weight):
    chips, _, rows, _ = x.shape
    shape = (chips * rows, weight.shape[1])
    vmem = pl.BlockSpec(memory_space=pltpu.VMEM)
    return pl.pallas_call(
        project_kernel,
        in_specs=[pl.BlockSpec(memory_space=pltpu.SMEM), vmem, vmem],
        out_specs=[vmem, vmem],
        out_shape=[
            jax.ShapeDtypeStruct(shape, jnp.float32),
            jax.ShapeDtypeStruct(shape, jnp.bfloat16),
        ],
        compiler_params=params(limit=SMALL_LIMIT),
        cost_estimate=pl.CostEstimate(
            flops=2 * x.size * weight.shape[1], bytes_accessed=4 * x.size, transcendentals=0
        ),
        name="project",
    )(core.astype(jnp.int32).reshape(1), x, weight)


def gate_up_kernel(x_ref, perm_ref, gain_ref, gate_hbm, up_hbm, out_ref, gate_ref, up_ref, sem):
    experts, _, width = gate_ref.shape
    count = x_ref.shape[0] // experts
    copies = [
        [
            pltpu.make_async_copy(gate_hbm.at[e], gate_ref.at[e], sem.at[0, e]),
            pltpu.make_async_copy(up_hbm.at[e], up_ref.at[e], sem.at[1, e]),
        ]
        for e in range(experts)
    ]
    for pair in copies:
        for copy in pair:
            copy.start()
    for e in range(experts):
        at = slice(e * count, (e + 1) * count)
        rows = jnp.dot(perm_ref[at, :], x_ref[...], preferred_element_type=jnp.float32)
        scaled = (rows * gain_ref[0:1, :]).astype(jnp.bfloat16)
        squares = jnp.sum(rows * rows, axis=1, keepdims=True)
        high, mid, _ = split_bf16(squares)
        lane = lax.broadcasted_iota(jnp.int32, (count, LANES), 1)
        pad = jnp.where(lane == 0, high.astype(jnp.float32), 0.0)
        pad = jnp.where(lane == 1, mid.astype(jnp.float32), pad)
        out_ref[at, 2 * width :] = pad.astype(jnp.bfloat16)
        copies[e][0].wait()
        out_ref[at, :width] = jnp.dot(
            scaled, gate_ref[e], preferred_element_type=jnp.float32
        ).astype(jnp.bfloat16)
        copies[e][1].wait()
        out_ref[at, width : 2 * width] = jnp.dot(
            scaled, up_ref[e], preferred_element_type=jnp.float32
        ).astype(jnp.bfloat16)


def gate_up(x, perm, gain, gate_proj, up_proj):
    experts, depth, ff = gate_proj.shape
    slots = x.shape[0]
    vmem = pl.BlockSpec(memory_space=pltpu.VMEM)
    anywhere = pl.BlockSpec(memory_space=pl.ANY)
    return pl.pallas_call(
        gate_up_kernel,
        in_specs=[vmem] * 3 + [anywhere] * 2,
        out_specs=vmem,
        out_shape=jax.ShapeDtypeStruct((slots, 2 * ff + LANES), jnp.bfloat16),
        scratch_shapes=[
            pltpu.VMEM(gate_proj.shape, jnp.bfloat16),
            pltpu.VMEM(up_proj.shape, jnp.bfloat16),
            pltpu.SemaphoreType.DMA((2, experts)),
        ],
        compiler_params=params(limit=LARGE_LIMIT),
        cost_estimate=pl.CostEstimate(
            flops=4 * slots * depth * ff,
            bytes_accessed=4 * experts * depth * ff + 4 * slots * ff,
            transcendentals=0,
        ),
        name="gate_up",
    )(x, perm, gain, gate_proj, up_proj)


def activate_kernel(x_ref, out_ref):
    parts, rows, ff = out_ref.shape
    squares = jnp.zeros((rows, 1), jnp.float32)
    for part in range(parts):
        pad = x_ref[part, :, 2 * ff :].astype(jnp.float32)
        squares = squares + pad[:, 0:1] + pad[:, 1:2]
    inv_rms = lax.rsqrt(squares / D + EPSILON)
    step = 256
    for at in range(0, ff, step):
        gate = jnp.zeros((rows, step), jnp.float32)
        up = jnp.zeros((rows, step), jnp.float32)
        for part in range(parts):
            gate = gate + x_ref[part, :, at : at + step].astype(jnp.float32)
            up = up + x_ref[part, :, ff + at : ff + at + step].astype(jnp.float32)
        gate = gate * inv_rms
        up = up * inv_rms
        result = (gate / (1.0 + jnp.exp(-gate)) * up).astype(jnp.bfloat16)
        for part in range(parts):
            out_ref[part, :, at : at + step] = result


def activate(parts):
    count, rows, width = parts.shape
    return pl.pallas_call(
        activate_kernel,
        out_shape=jax.ShapeDtypeStruct((count, rows, (width - LANES) // 2), jnp.bfloat16),
        compiler_params=params(limit=SMALL_LIMIT),
        name="activate",
    )(parts)


def down_kernel(act_ref, back_ref, down_hbm, out_ref, all_ref, down_ref, sem):
    experts = down_ref.shape[0]
    count = act_ref.shape[0] // experts
    copies = [
        pltpu.make_async_copy(down_hbm.at[e], down_ref.at[e], sem.at[e]) for e in range(experts)
    ]
    for copy in copies:
        copy.start()
    for e in range(experts):
        at = slice(e * count, (e + 1) * count)
        copies[e].wait()
        all_ref[at, :] = jnp.dot(
            act_ref[at, :], down_ref[e], preferred_element_type=jnp.float32
        ).astype(jnp.bfloat16)
    out_ref[...] = jnp.dot(
        back_ref[...], all_ref[...], preferred_element_type=jnp.float32
    ).astype(jnp.bfloat16)


def down(act, back, down_proj):
    experts, ff, width = down_proj.shape
    slots = act.shape[0]
    vmem = pl.BlockSpec(memory_space=pltpu.VMEM)
    return pl.pallas_call(
        down_kernel,
        in_specs=[vmem] * 2 + [pl.BlockSpec(memory_space=pl.ANY)],
        out_specs=vmem,
        out_shape=jax.ShapeDtypeStruct((slots, width), jnp.bfloat16),
        scratch_shapes=[
            pltpu.VMEM((slots, width), jnp.bfloat16),
            pltpu.VMEM(down_proj.shape, jnp.bfloat16),
            pltpu.SemaphoreType.DMA((experts,)),
        ],
        compiler_params=params(limit=LARGE_LIMIT),
        cost_estimate=pl.CostEstimate(
            flops=2 * slots * ff * width,
            bytes_accessed=2 * experts * ff * width,
            transcendentals=0,
        ),
        name="down",
    )(act, back, down_proj)


def per_device(
    queries,
    tree_key_cache,
    tree_value_cache,
    tree_mask,
    lengths,
    out_weight,
    residual,
    norm_gain,
    expert_ids,
    gate_weights,
    gate_proj,
    up_proj,
    down_proj,
):
    rows = queries.shape[0]
    blocks, part_tokens = tree_key_cache.shape[:2]
    n_blk = lax.axis_size(BLK)
    n_narrow = lax.axis_size(NARROW)
    zl, x, core = (lax.axis_index(name) for name in BLK)
    zh, yh, yl = (lax.axis_index(name) for name in NARROW)
    kv_head = yh * 2 + yl
    heads = QUERY_HEADS // n_narrow
    width = heads * HEAD_SIZE
    swap = [(0, 1), (1, 0)]
    size_x = lax.axis_size("x")

    def head_piece(head):
        at = head * HEAD_SIZE
        return jnp.stack(
            [
                lax.dynamic_slice_in_dim(cache, at, HEAD_SIZE, 2)
                for cache in (tree_key_cache, tree_value_cache)
            ]
        )

    pieces = [head_piece(kv_head ^ step) for step in range(KEY_VALUE_HEADS)]
    kv = [pieces[0]]
    for step in (1, 3, 2):
        pairs = [(i, i ^ step) for i in range(KEY_VALUE_HEADS)]
        kv.append(lax.ppermute(pieces[step], ("yh", "yl"), pairs))
    kv = kv + [lax.ppermute(piece, "core", swap) for piece in kv]
    sources = [zh * KEY_VALUE_HEADS + (kv_head ^ s) for s in (0, 1, 3, 2)]

    both = lax.dynamic_slice_in_dim(queries, kv_head * 2 * width, 2 * width, 1)
    both = both.reshape(rows, 2, 2, width // 2)
    extra = jnp.concatenate(
        [
            tree_mask.astype(jnp.bfloat16),
            (lengths // 256).astype(jnp.bfloat16)[:, None],
            (lengths % 256).astype(jnp.bfloat16)[:, None],
            jnp.zeros((rows, LANES - TREE_BLOCKS - 2), jnp.bfloat16) + pieces[1][0, 0, 0, 0] * 0,
        ],
        axis=1,
    )
    own_q = lax.dynamic_index_in_dim(both, core, 2, False).reshape(rows, width)
    other_q = lax.dynamic_index_in_dim(both, 1 - core, 2, False).reshape(rows, width)
    own_q = jnp.concatenate([own_q, extra], axis=1)
    other_q = lax.ppermute(jnp.concatenate([other_q, extra], axis=1), "core", swap)
    pair = jnp.concatenate([own_q, other_q], axis=0)
    far = lax.ppermute(pair, "zl", swap)
    pair = jnp.concatenate([pair, far], axis=0)

    all_q, groups = [pair], []
    for dx in (0, 2, 1, 3):
        if dx:
            pairs = [(i, (i + dx) % size_x) for i in range(size_x)]
            all_q.append(lax.ppermute(pair, "x", pairs))
        for dz in range(2):
            origin = (zl ^ dz) * size_x + (x - dx) % size_x
            groups += [origin * 2 + core, origin * 2 + (1 - core)]
    zero = jnp.int32(0)
    info = [zl * size_x + x, core, zero, zero] + sources + groups
    info = jnp.stack([value.astype(jnp.int32) for value in info])
    group_axes = ("zl", "x", "zh")
    partial = attention(info, all_q, kv)
    partial = lax.all_to_all(partial.reshape(n_blk, rows, width + LANES), group_axes, 0, 0)
    attended = combine(partial, heads)

    gathered = jnp.zeros((KEY_VALUE_HEADS,) + attended.shape, attended.dtype)
    gathered = lax.dynamic_update_index_in_dim(gathered, attended, kv_head, 0)
    for step in range(1, KEY_VALUE_HEADS):
        pairs = [(i, i ^ step) for i in range(KEY_VALUE_HEADS)]
        piece = lax.ppermute(attended, ("yh", "yl"), pairs)
        gathered = lax.dynamic_update_index_in_dim(gathered, piece, kv_head ^ step, 0)
    gathered = gathered.reshape(n_blk // 2, 1, rows, -1)
    gathered = jnp.broadcast_to(gathered, (n_blk // 2, 2) + gathered.shape[2:])
    gathered = lax.all_to_all(gathered.reshape((n_blk,) + gathered.shape[2:]), group_axes, 0, 0)
    mine, other = project(core, gathered.reshape(n_blk // 2, 2, rows, -1), out_weight)
    projected = (mine + lax.ppermute(other, "core", swap).astype(jnp.float32)).astype(jnp.bfloat16)
    projected = projected.reshape(n_blk // 2, rows, -1)
    projected = lax.all_to_all(projected, ("zl", "x"), 0, 0)
    projected = jnp.sum(projected.astype(jnp.float32), axis=0)
    hidden_b = (residual.astype(jnp.float32) + projected).astype(jnp.bfloat16)

    exp_dev = gate_proj.shape[0]
    n_experts = exp_dev * n_blk
    flat_ids = expert_ids.reshape(-1)
    expert_hot = (flat_ids[:, None] == jnp.arange(n_experts)[None, :]).astype(jnp.int32)
    earlier = jnp.cumsum(expert_hot, axis=0) - expert_hot
    slot_of = jnp.sum(earlier * expert_hot, axis=1)
    target = (flat_ids * CAP + slot_of).reshape(rows, TOP)
    slots = n_experts * CAP
    at_slot = target[:, :, None] == jnp.arange(slots)[None, None, :]
    select = jnp.any(at_slot, axis=1).astype(jnp.bfloat16)
    mixing = jnp.sum(jnp.where(at_slot, gate_weights[:, :, None], 0.0), axis=1)
    outgoing = lax.dot_general(
        select, hidden_b, (((0,), (0,)), ((), ())), preferred_element_type=jnp.float32
    ).astype(jnp.bfloat16)
    incoming = lax.all_to_all(outgoing.reshape(n_blk, exp_dev * CAP, -1), BLK, 0, 0)

    place = jnp.arange(slots)
    expert, rest = place // (n_blk * CAP), place % (n_blk * CAP)
    order = (rest // CAP) * (exp_dev * CAP) + expert * CAP + rest % CAP
    perm = (order[:, None] == place[None, :]).astype(jnp.bfloat16)

    back = (place[:, None] == order[None, :]).astype(jnp.bfloat16)
    gain = jnp.broadcast_to(norm_gain[None], (8, norm_gain.shape[0])) + perm[0, 1] * 0
    sums = gate_up(
        incoming.reshape(slots, -1), perm, gain, gate_proj, up_proj
    )
    sums = lax.all_to_all(sums.reshape(n_narrow, slots // n_narrow, -1), NARROW, 0, 0)
    activated = activate(sums)
    activated = lax.all_to_all(activated, NARROW, 0, 0).reshape(slots, -1)
    expert_out = down(activated, back, down_proj)
    returned = lax.all_to_all(expert_out.reshape(n_blk, exp_dev * CAP, -1), BLK, 0, 0)
    returned = returned.reshape(slots, -1)
    mix_high = lax.reduce_precision(mixing, 8, 7)
    mix_low = mixing - mix_high
    mixed_in = jnp.dot(
        mix_high.astype(jnp.bfloat16), returned, preferred_element_type=jnp.float32
    ) + jnp.dot(mix_low.astype(jnp.bfloat16), returned, preferred_element_type=jnp.float32)
    return (hidden_b.astype(jnp.float32) + mixed_in).astype(jnp.bfloat16)


def solution(mesh):
    shape = (2, 4, 2, 2, 2, 2)
    fine = Mesh(mesh.devices.reshape(shape), BLK + NARROW)
    in_specs = (
        P(BLK, None),
        P(BLK, NARROW, None),
        P(BLK, NARROW, None),
        P(BLK, None),
        P(BLK),
        P(BLK, NARROW),
        P(BLK, NARROW),
        P(NARROW),
        P(BLK, None),
        P(BLK, None),
        P(BLK, NARROW, None),
        P(BLK, NARROW, None),
        P(BLK, None, NARROW),
    )
    out_specs = P(BLK, NARROW)
    return jax.shard_map(
        per_device, mesh=fine, in_specs=in_specs, out_specs=out_specs, check_vma=False
    )
```

```python
import functools

import jax
import jax.numpy as jnp
from jax import lax
from jax.experimental import pallas as pl
from jax.experimental.pallas import tpu as pltpu
from jax.sharding import Mesh
from jax.sharding import PartitionSpec as P

D = 4096
QUERY_HEADS = 64
KEY_VALUE_HEADS = 4
HEAD_SIZE = 128
FF = 1536
TOP = 8
CAP = 6
BLOCK_TOKENS = 1024
TREE_BLOCKS = 64
NEGATIVE_FILLER = -1e30
EPSILON = 1e-06
SCORE_SCALE = HEAD_SIZE ** (-0.5)
LOG2E = 1.4426950408889634
LANES = 128
BLK = ("zl", "x", "core")
NARROW = ("zh", "yh", "yl")
SAFE_POWER = 100.0
VMEM_LIMIT = 40 * 1024 * 1024
LARGE_LIMIT = 56 * 1024 * 1024
SMALL_LIMIT = 12 * 1024 * 1024


def params(limit):
    return pltpu.CompilerParams(vmem_limit_bytes=limit)


def split_bf16(value):
    high = value.astype(jnp.bfloat16)
    rest = value - high.astype(jnp.float32)
    mid = rest.astype(jnp.bfloat16)
    low = (rest - mid.astype(jnp.float32)).astype(jnp.bfloat16)
    return high, mid, low


def attention_kernel(heads, info_ref, *refs):
    q_in = refs[0:4]
    kv_in = refs[4:12]
    out_ref, q_ref, k_ref, v_ref, vt_ref, lim_ref, mask_ref, s_ref, lse_ref, sem = refs[12:]
    rows = q_ref.shape[0]
    base = heads * HEAD_SIZE
    chip, core = info_ref[0], info_ref[1]
    chip_blocks, sources = k_ref.shape[:2]
    blocks = chip_blocks // 2
    span = sources * LANES
    tokens = chip_blocks * span
    step = rows // len(q_in)
    factor = SCORE_SCALE * LOG2E

    copies = []
    for i, ref in enumerate(q_in):
        at = pl.ds(i * step, step)
        copies.append(pltpu.make_async_copy(ref, q_ref.at[at], sem.at[len(copies)]))
    for i, ref in enumerate(kv_in):
        side, s = i // sources, i % sources
        for part, target in enumerate((k_ref, v_ref)):
            to = target.at[pl.ds(side * blocks, blocks), s]
            copies.append(pltpu.make_async_copy(ref.at[part], to, sem.at[len(copies)]))
    for copy in copies:
        copy.start()

    sub = lax.broadcasted_iota(jnp.int32, (16, tokens), 0)
    vt_ref[HEAD_SIZE:, :] = jnp.where(sub == 0, 1.0, 0.0).astype(jnp.bfloat16)
    for copy in copies[: len(q_in)]:
        copy.wait()
    extra = q_ref[:, base:].astype(jnp.float32).T
    lim_ref[...] = extra
    length = extra[TREE_BLOCKS : TREE_BLOCKS + 1] * 256.0 + extra[TREE_BLOCKS + 1 : TREE_BLOCKS + 2]
    first = pl.multiple_of(chip * chip_blocks, chip_blocks)
    reads = lim_ref[pl.ds(first, chip_blocks), :]
    block_id = lax.broadcasted_iota(jnp.int32, (chip_blocks, rows), 0) + first
    bound = length - (block_id * BLOCK_TOKENS).astype(jnp.float32)
    lim_ref[0:chip_blocks, :] = jnp.where(reads > 0.5, bound, 0.0)
    most_q = jnp.zeros((rows, 1), jnp.float32)
    for h in range(heads):
        q = q_ref[:, h * HEAD_SIZE : (h + 1) * HEAD_SIZE].astype(jnp.float32)
        most_q = jnp.maximum(most_q, jnp.sum(q * q, axis=1, keepdims=True))
    token = lax.broadcasted_iota(jnp.int32, (LANES, 1), 0)
    token = [(token + info_ref[4 + s] * LANES).astype(jnp.float32) for s in range(sources)]
    token = jnp.concatenate(token, axis=0)
    for i in range(chip_blocks):
        at = slice(i * span, (i + 1) * span)
        side = core if i < blocks else 1 - core
        lim = lim_ref[pl.ds(side * blocks + i % blocks, 1), :]
        mask_ref[at, :] = jnp.where(token < lim, 1.0, 0.0).astype(jnp.bfloat16)
    for copy in copies[len(q_in) :]:
        copy.wait()
    most_k = jnp.zeros((LANES, HEAD_SIZE), jnp.float32)
    for i in range(chip_blocks):
        vt_ref[:HEAD_SIZE, i * span : (i + 1) * span] = v_ref[i].reshape(span, HEAD_SIZE).T
        for s in range(sources):
            keys = k_ref[i, s].astype(jnp.float32)
            most_k = jnp.maximum(most_k, keys * keys)
    most_k = jnp.sum(jnp.max(most_k, axis=0, keepdims=True), axis=1, keepdims=True)
    most = jnp.max(most_q) * jnp.max(most_k) * (factor * factor)
    small = most <= SAFE_POWER * SAFE_POWER

    def finish(h, cols, acc, top):
        total = acc[HEAD_SIZE : HEAD_SIZE + 1]
        some = total > 0
        safe = jnp.where(some, total, 1.0)
        result = (acc[:HEAD_SIZE] / safe).astype(jnp.bfloat16).T
        group = rows // 16
        for i in range(16):
            row = pl.multiple_of(info_ref[8 + i] * group, group)
            out_ref[pl.ds(row, group), cols] = result[i * group : (i + 1) * group]
        lse = jnp.where(some, top * SCORE_SCALE + jnp.log(safe), NEGATIVE_FILLER)
        lse_ref[pl.ds(h, 1), :] = lse

    def head_columns(h):
        return pl.ds(pl.multiple_of(h * HEAD_SIZE, HEAD_SIZE), HEAD_SIZE)

    chunk = 4

    def small_head(h, carry):
        cols = head_columns(h)
        qt = q_ref[:, cols].T
        acc = jnp.zeros((HEAD_SIZE + 16, rows), jnp.float32)
        for i in range(0, chip_blocks, chunk):
            at = slice(i * span, (i + chunk) * span)
            keys = k_ref[i : i + chunk].reshape(chunk * span, HEAD_SIZE)
            s = jnp.dot(keys, qt, preferred_element_type=jnp.float32) * factor
            p = jnp.exp2(s).astype(jnp.bfloat16) * mask_ref[at, :]
            acc = acc + jnp.dot(vt_ref[:, at], p, preferred_element_type=jnp.float32)
        finish(h, cols, acc, 0.0)
        return carry

    def any_head(h, carry):
        cols = head_columns(h)
        qt = q_ref[:, cols].T
        top = jnp.full((1, rows), -1e29, jnp.float32)
        for i in range(chip_blocks):
            at = slice(i * span, (i + 1) * span)
            keys = k_ref[i].reshape(span, HEAD_SIZE)
            s = jnp.dot(keys, qt, preferred_element_type=jnp.float32)
            s = jnp.where(mask_ref[at, :].astype(jnp.float32) > 0.5, s, NEGATIVE_FILLER)
            s_ref[at, :] = s
            top = jnp.maximum(top, jnp.max(s, axis=0, keepdims=True))
        acc = jnp.zeros((HEAD_SIZE + 16, rows), jnp.float32)
        for i in range(chip_blocks):
            at = slice(i * span, (i + 1) * span)
            p = jnp.exp2((s_ref[at, :] - top) * factor).astype(jnp.bfloat16)
            acc = acc + jnp.dot(vt_ref[:, at], p, preferred_element_type=jnp.float32)
        finish(h, cols, acc, top)
        return carry

    @pl.when(small)
    def _():
        lax.fori_loop(0, heads, small_head, 0, unroll=2)

    @pl.when(jnp.logical_not(small))
    def _():
        lax.fori_loop(0, heads, any_head, 0)

    high, mid, low = split_bf16(lse_ref[...])
    pieces = [piece.astype(jnp.float32) for piece in (high, mid, low)]
    pieces.append(jnp.zeros((LANES - 3 * heads, rows), jnp.float32))
    result = jnp.concatenate(pieces, axis=0).T.astype(jnp.bfloat16)
    group = rows // 16
    for i in range(16):
        row = pl.multiple_of(info_ref[8 + i] * group, group)
        out_ref[pl.ds(row, group), base:] = result[i * group : (i + 1) * group]


def attention(info, queries, kv):
    step, width = queries[0].shape
    rows = step * len(queries)
    heads = (width - LANES) // HEAD_SIZE
    blocks = kv[0].shape[1]
    sources = len(kv) // 2
    tokens = len(kv) * blocks * LANES
    anywhere = pl.BlockSpec(memory_space=pl.ANY)
    tiles = (2 * blocks, sources, LANES, HEAD_SIZE)
    return pl.pallas_call(
        functools.partial(attention_kernel, heads),
        in_specs=[pl.BlockSpec(memory_space=pltpu.SMEM)] + [anywhere] * (len(queries) + len(kv)),
        out_specs=pl.BlockSpec(memory_space=pltpu.VMEM),
        out_shape=jax.ShapeDtypeStruct((rows, width), jnp.bfloat16),
        scratch_shapes=[
            pltpu.VMEM((rows, width), jnp.bfloat16),
            pltpu.VMEM(tiles, jnp.bfloat16),
            pltpu.VMEM(tiles, jnp.bfloat16),
            pltpu.VMEM((HEAD_SIZE + 16, tokens), jnp.bfloat16),
            pltpu.VMEM((LANES, rows), jnp.float32),
            pltpu.VMEM((tokens, rows), jnp.bfloat16),
            pltpu.VMEM((tokens, rows), jnp.float32),
            pltpu.VMEM((heads, rows), jnp.float32),
            pltpu.SemaphoreType.DMA((len(queries) + 2 * len(kv),)),
        ],
        compiler_params=params(limit=VMEM_LIMIT),
        cost_estimate=pl.CostEstimate(
            flops=6 * rows * heads * tokens * HEAD_SIZE,
            bytes_accessed=6 << 20,
            transcendentals=rows * heads * tokens,
        ),
        name="attention",
    )(info, *queries, *kv)


def combine_kernel(heads, x_ref, out_ref):
    base = heads * HEAD_SIZE
    info = x_ref[:, :, base:].astype(jnp.float32)
    for h in range(heads):
        lse = info[:, :, h : h + 1] + info[:, :, 8 + h : 9 + h]
        lse = lse + info[:, :, 16 + h : 17 + h]
        scale = jnp.exp(lse - jnp.max(lse, axis=0, keepdims=True))
        cols = slice(h * HEAD_SIZE, (h + 1) * HEAD_SIZE)
        acc = jnp.sum(x_ref[:, :, cols].astype(jnp.float32) * scale, axis=0)
        at = h % (heads // 2) * HEAD_SIZE
        out_ref[h // (heads // 2), :, at : at + HEAD_SIZE] = (
            acc / jnp.sum(scale, axis=0)
        ).astype(jnp.bfloat16)


def combine(parts, heads):
    _, rows, _ = parts.shape
    return pl.pallas_call(
        functools.partial(combine_kernel, heads),
        out_shape=jax.ShapeDtypeStruct((2, rows, heads * HEAD_SIZE // 2), jnp.bfloat16),
        compiler_params=params(limit=SMALL_LIMIT),
        cost_estimate=pl.CostEstimate(
            flops=4 * parts.size, bytes_accessed=2 * parts.size, transcendentals=0
        ),
        name="combine",
    )(parts)


def project_kernel(core_ref, x_ref, weight_ref, mine_ref, other_ref):
    chips, _, rows, depth = x_ref.shape
    core = core_ref[0]
    for ref, side in ((other_ref, 1 - core), (mine_ref, core)):
        x = x_ref[:, pl.ds(side, 1)].reshape(chips * rows, depth)
        product = jnp.dot(x, weight_ref[...], preferred_element_type=jnp.float32)
        ref[...] = product.astype(ref.dtype)


def project(core, x, weight):
    chips, _, rows, _ = x.shape
    shape = (chips * rows, weight.shape[1])
    vmem = pl.BlockSpec(memory_space=pltpu.VMEM)
    return pl.pallas_call(
        project_kernel,
        in_specs=[pl.BlockSpec(memory_space=pltpu.SMEM), vmem, vmem],
        out_specs=[vmem, vmem],
        out_shape=[
            jax.ShapeDtypeStruct(shape, jnp.float32),
            jax.ShapeDtypeStruct(shape, jnp.bfloat16),
        ],
        compiler_params=params(limit=SMALL_LIMIT),
        cost_estimate=pl.CostEstimate(
            flops=2 * x.size * weight.shape[1], bytes_accessed=4 * x.size, transcendentals=0
        ),
        name="project",
    )(core.astype(jnp.int32).reshape(1), x, weight)


def gate_up_kernel(x_ref, perm_ref, gain_ref, gate_hbm, up_hbm, out_ref, gate_ref, up_ref, sem):
    experts, _, width = gate_ref.shape
    count = x_ref.shape[0] // experts
    copies = [
        [
            pltpu.make_async_copy(gate_hbm.at[e], gate_ref.at[e], sem.at[0, e]),
            pltpu.make_async_copy(up_hbm.at[e], up_ref.at[e], sem.at[1, e]),
        ]
        for e in range(experts)
    ]
    for pair in copies:
        for copy in pair:
            copy.start()
    for e in range(experts):
        at = slice(e * count, (e + 1) * count)
        rows = jnp.dot(perm_ref[at, :], x_ref[...], preferred_element_type=jnp.float32)
        scaled = (rows * gain_ref[0:1, :]).astype(jnp.bfloat16)
        squares = jnp.sum(rows * rows, axis=1, keepdims=True)
        high, mid, _ = split_bf16(squares)
        lane = lax.broadcasted_iota(jnp.int32, (count, LANES), 1)
        pad = jnp.where(lane == 0, high.astype(jnp.float32), 0.0)
        pad = jnp.where(lane == 1, mid.astype(jnp.float32), pad)
        out_ref[at, 2 * width :] = pad.astype(jnp.bfloat16)
        copies[e][0].wait()
        out_ref[at, :width] = jnp.dot(
            scaled, gate_ref[e], preferred_element_type=jnp.float32
        ).astype(jnp.bfloat16)
        copies[e][1].wait()
        out_ref[at, width : 2 * width] = jnp.dot(
            scaled, up_ref[e], preferred_element_type=jnp.float32
        ).astype(jnp.bfloat16)


def gate_up(x, perm, gain, gate_proj, up_proj):
    experts, depth, ff = gate_proj.shape
    slots = x.shape[0]
    vmem = pl.BlockSpec(memory_space=pltpu.VMEM)
    anywhere = pl.BlockSpec(memory_space=pl.ANY)
    return pl.pallas_call(
        gate_up_kernel,
        in_specs=[vmem] * 3 + [anywhere] * 2,
        out_specs=vmem,
        out_shape=jax.ShapeDtypeStruct((slots, 2 * ff + LANES), jnp.bfloat16),
        scratch_shapes=[
            pltpu.VMEM(gate_proj.shape, jnp.bfloat16),
            pltpu.VMEM(up_proj.shape, jnp.bfloat16),
            pltpu.SemaphoreType.DMA((2, experts)),
        ],
        compiler_params=params(limit=LARGE_LIMIT),
        cost_estimate=pl.CostEstimate(
            flops=4 * slots * depth * ff,
            bytes_accessed=4 * experts * depth * ff + 4 * slots * ff,
            transcendentals=0,
        ),
        name="gate_up",
    )(x, perm, gain, gate_proj, up_proj)


def activate_kernel(x_ref, out_ref):
    parts, rows, ff = out_ref.shape
    squares = jnp.zeros((rows, 1), jnp.float32)
    for part in range(parts):
        pad = x_ref[part, :, 2 * ff :].astype(jnp.float32)
        squares = squares + pad[:, 0:1] + pad[:, 1:2]
    inv_rms = lax.rsqrt(squares / D + EPSILON)
    step = 256
    for at in range(0, ff, step):
        gate = jnp.zeros((rows, step), jnp.float32)
        up = jnp.zeros((rows, step), jnp.float32)
        for part in range(parts):
            gate = gate + x_ref[part, :, at : at + step].astype(jnp.float32)
            up = up + x_ref[part, :, ff + at : ff + at + step].astype(jnp.float32)
        gate = gate * inv_rms
        up = up * inv_rms
        result = (gate / (1.0 + jnp.exp(-gate)) * up).astype(jnp.bfloat16)
        for part in range(parts):
            out_ref[part, :, at : at + step] = result


def activate(parts):
    count, rows, width = parts.shape
    return pl.pallas_call(
        activate_kernel,
        out_shape=jax.ShapeDtypeStruct((count, rows, (width - LANES) // 2), jnp.bfloat16),
        compiler_params=params(limit=SMALL_LIMIT),
        name="activate",
    )(parts)


def down_kernel(act_ref, back_ref, down_hbm, out_ref, all_ref, down_ref, sem):
    experts = down_ref.shape[0]
    count = act_ref.shape[0] // experts
    copies = [
        pltpu.make_async_copy(down_hbm.at[e], down_ref.at[e], sem.at[e]) for e in range(experts)
    ]
    for copy in copies:
        copy.start()
    for e in range(experts):
        at = slice(e * count, (e + 1) * count)
        copies[e].wait()
        all_ref[at, :] = jnp.dot(
            act_ref[at, :], down_ref[e], preferred_element_type=jnp.float32
        ).astype(jnp.bfloat16)
    out_ref[...] = jnp.dot(
        back_ref[...], all_ref[...], preferred_element_type=jnp.float32
    ).astype(jnp.bfloat16)


def down(act, back, down_proj):
    experts, ff, width = down_proj.shape
    slots = act.shape[0]
    vmem = pl.BlockSpec(memory_space=pltpu.VMEM)
    return pl.pallas_call(
        down_kernel,
        in_specs=[vmem] * 2 + [pl.BlockSpec(memory_space=pl.ANY)],
        out_specs=vmem,
        out_shape=jax.ShapeDtypeStruct((slots, width), jnp.bfloat16),
        scratch_shapes=[
            pltpu.VMEM((slots, width), jnp.bfloat16),
            pltpu.VMEM(down_proj.shape, jnp.bfloat16),
            pltpu.SemaphoreType.DMA((experts,)),
        ],
        compiler_params=params(limit=LARGE_LIMIT),
        cost_estimate=pl.CostEstimate(
            flops=2 * slots * ff * width,
            bytes_accessed=2 * experts * ff * width,
            transcendentals=0,
        ),
        name="down",
    )(act, back, down_proj)


def per_device(
    queries,
    tree_key_cache,
    tree_value_cache,
    tree_mask,
    lengths,
    out_weight,
    residual,
    norm_gain,
    expert_ids,
    gate_weights,
    gate_proj,
    up_proj,
    down_proj,
):
    rows = queries.shape[0]
    blocks, part_tokens = tree_key_cache.shape[:2]
    n_blk = lax.axis_size(BLK)
    n_narrow = lax.axis_size(NARROW)
    zl, x, core = (lax.axis_index(name) for name in BLK)
    zh, yh, yl = (lax.axis_index(name) for name in NARROW)
    kv_head = yh * 2 + yl
    heads = QUERY_HEADS // n_narrow
    width = heads * HEAD_SIZE
    swap = [(0, 1), (1, 0)]
    size_x = lax.axis_size("x")

    def head_piece(head):
        at = head * HEAD_SIZE
        return jnp.stack(
            [
                lax.dynamic_slice_in_dim(cache, at, HEAD_SIZE, 2)
                for cache in (tree_key_cache, tree_value_cache)
            ]
        )

    pieces = [head_piece(kv_head ^ step) for step in range(KEY_VALUE_HEADS)]
    kv = [pieces[0]]
    for step in (1, 3, 2):
        pairs = [(i, i ^ step) for i in range(KEY_VALUE_HEADS)]
        kv.append(lax.ppermute(pieces[step], ("yh", "yl"), pairs))
    kv = kv + [lax.ppermute(piece, "core", swap) for piece in kv]
    sources = [zh * KEY_VALUE_HEADS + (kv_head ^ s) for s in (0, 1, 3, 2)]

    both = lax.dynamic_slice_in_dim(queries, kv_head * 2 * width, 2 * width, 1)
    both = both.reshape(rows, 2, 2, width // 2)
    extra = jnp.concatenate(
        [
            tree_mask.astype(jnp.bfloat16),
            (lengths // 256).astype(jnp.bfloat16)[:, None],
            (lengths % 256).astype(jnp.bfloat16)[:, None],
            jnp.zeros((rows, LANES - TREE_BLOCKS - 2), jnp.bfloat16) + pieces[1][0, 0, 0, 0] * 0,
        ],
        axis=1,
    )
    own_q = lax.dynamic_index_in_dim(both, core, 2, False).reshape(rows, width)
    other_q = lax.dynamic_index_in_dim(both, 1 - core, 2, False).reshape(rows, width)
    own_q = jnp.concatenate([own_q, extra], axis=1)
    other_q = lax.ppermute(jnp.concatenate([other_q, extra], axis=1), "core", swap)
    pair = jnp.concatenate([own_q, other_q], axis=0)
    far = lax.ppermute(pair, "zl", swap)
    pair = jnp.concatenate([pair, far], axis=0)

    all_q, groups = [pair], []
    for dx in (0, 2, 1, 3):
        if dx:
            pairs = [(i, (i + dx) % size_x) for i in range(size_x)]
            all_q.append(lax.ppermute(pair, "x", pairs))
        for dz in range(2):
            origin = (zl ^ dz) * size_x + (x - dx) % size_x
            groups += [origin * 2 + core, origin * 2 + (1 - core)]
    zero = jnp.int32(0)
    info = [zl * size_x + x, core, zero, zero] + sources + groups
    info = jnp.stack([value.astype(jnp.int32) for value in info])
    group_axes = ("zl", "x", "zh")
    partial = attention(info, all_q, kv)
    partial = lax.all_to_all(partial.reshape(n_blk, rows, width + LANES), group_axes, 0, 0)
    attended = combine(partial, heads)

    gathered = jnp.broadcast_to(attended[None], (KEY_VALUE_HEADS,) + attended.shape)
    gathered = lax.all_to_all(gathered, ("yh", "yl"), 0, 0)
    gathered = gathered.reshape(n_blk // 2, 1, rows, -1)
    gathered = jnp.broadcast_to(gathered, (n_blk // 2, 2) + gathered.shape[2:])
    gathered = lax.all_to_all(gathered.reshape((n_blk,) + gathered.shape[2:]), group_axes, 0, 0)
    mine, other = project(core, gathered.reshape(n_blk // 2, 2, rows, -1), out_weight)
    projected = (mine + lax.ppermute(other, "core", swap).astype(jnp.float32)).astype(jnp.bfloat16)
    projected = projected.reshape(n_blk // 2, rows, -1)
    projected = lax.all_to_all(projected, ("zl", "x"), 0, 0)
    projected = jnp.sum(projected.astype(jnp.float32), axis=0)
    hidden_b = (residual.astype(jnp.float32) + projected).astype(jnp.bfloat16)

    exp_dev = gate_proj.shape[0]
    n_experts = exp_dev * n_blk
    flat_ids = expert_ids.reshape(-1)
    expert_hot = (flat_ids[:, None] == jnp.arange(n_experts)[None, :]).astype(jnp.int32)
    earlier = jnp.cumsum(expert_hot, axis=0) - expert_hot
    slot_of = jnp.sum(earlier * expert_hot, axis=1)
    target = (flat_ids * CAP + slot_of).reshape(rows, TOP)
    slots = n_experts * CAP
    at_slot = target[:, :, None] == jnp.arange(slots)[None, None, :]
    select = jnp.any(at_slot, axis=1).astype(jnp.bfloat16)
    mixing = jnp.sum(jnp.where(at_slot, gate_weights[:, :, None], 0.0), axis=1)
    outgoing = lax.dot_general(
        select, hidden_b, (((0,), (0,)), ((), ())), preferred_element_type=jnp.float32
    ).astype(jnp.bfloat16)
    incoming = lax.all_to_all(outgoing.reshape(n_blk, exp_dev * CAP, -1), BLK, 0, 0)

    place = jnp.arange(slots)
    expert, rest = place // (n_blk * CAP), place % (n_blk * CAP)
    order = (rest // CAP) * (exp_dev * CAP) + expert * CAP + rest % CAP
    perm = (order[:, None] == place[None, :]).astype(jnp.bfloat16)

    back = (place[:, None] == order[None, :]).astype(jnp.bfloat16)
    gain = jnp.broadcast_to(norm_gain[None], (8, norm_gain.shape[0])) + perm[0, 1] * 0
    sums = gate_up(
        incoming.reshape(slots, -1), perm, gain, gate_proj, up_proj
    )
    sums = lax.all_to_all(sums.reshape(n_narrow, slots // n_narrow, -1), NARROW, 0, 0)
    activated = activate(sums)
    activated = lax.all_to_all(activated, NARROW, 0, 0).reshape(slots, -1)
    expert_out = down(activated, back, down_proj)
    returned = lax.all_to_all(expert_out.reshape(n_blk, exp_dev * CAP, -1), BLK, 0, 0)
    returned = returned.reshape(slots, -1)
    mix_high = lax.reduce_precision(mixing, 8, 7)
    mix_low = mixing - mix_high
    mixed_in = jnp.dot(
        mix_high.astype(jnp.bfloat16), returned, preferred_element_type=jnp.float32
    ) + jnp.dot(mix_low.astype(jnp.bfloat16), returned, preferred_element_type=jnp.float32)
    return (hidden_b.astype(jnp.float32) + mixed_in).astype(jnp.bfloat16)


def solution(mesh):
    shape = (2, 4, 2, 2, 2, 2)
    fine = Mesh(mesh.devices.reshape(shape), BLK + NARROW)
    in_specs = (
        P(BLK, None),
        P(BLK, NARROW, None),
        P(BLK, NARROW, None),
        P(BLK, None),
        P(BLK),
        P(BLK, NARROW),
        P(BLK, NARROW),
        P(NARROW),
        P(BLK, None),
        P(BLK, None),
        P(BLK, NARROW, None),
        P(BLK, NARROW, None),
        P(BLK, None, NARROW),
    )
    out_specs = P(BLK, NARROW)
    return jax.shard_map(
        per_device, mesh=fine, in_specs=in_specs, out_specs=out_specs, check_vma=False
    )
```
